32 devices in a mesh: mesh: 8 (over y, x, core), event: 4 (over z).
Axes of the slice: x: 2, y: 2, z: 4, core: 2. Of those that a mesh axis runs over, the one named last changes fastest.
Arguments:
- forward_now: float32 [4, 3, 20808], P('event', None, 'mesh'), may hold values from -6 to 6
- forward_prev: float32 [4, 3, 20808], P('event', None, 'mesh'), may hold values from -6 to 6
- adjoint_now: float32 [4, 3, 20808], P('event', None, 'mesh'), may hold values from -6 to 6
- adjoint_prev: float32 [4, 3, 20808], P('event', None, 'mesh'), may hold values from -6 to 6
- connectivity: int32 [125, 256], P(None, 'mesh'), may hold values from 0 to 2600, as said below
- lower_face: int32 [8, 289], P('mesh'), may hold values from 0 to 2600, as said below
- upper_face: int32 [8, 289], P('mesh'), may hold values from 0 to 2600, as said below
- bulk_modulus: float32 [125, 256], P(None, 'mesh'), may hold values from 0.5 to 2
- shear_modulus: float32 [125, 256], P(None, 'mesh'), may hold values from 0.3 to 1.2
- step_scale: float32 [20808], P('mesh'), may hold values from 0.0069 to 5.01, as said below
- receiver_points: int32 [1024], P('mesh'), may hold values from 0 to 2600
- adjoint_source: float32 [4, 2, 3, 1024], P('event', None, None, 'mesh'), may hold values from -18 to 18
Outputs:
- forward_next: float32 [4, 3, 20808], P('event', None, 'mesh')
- adjoint_next: float32 [4, 3, 20808], P('event', None, 'mesh')
- kernels: float32 [2, 125, 256], P(None, None, ('mesh', 'event'))
The draws below stay inside these ranges and needn't reach their ends.
Inputs may be any that keep to these rules, and one draw needn't show every extreme that they name: `connectivity`: each column lists local point numbers of its element's partition; every local point is used. A partition's elements come in 2 layers of 16: the first layer holds every point of the partition's lower_face, the last layer every point of its upper_face, and no other element touches those points. `lower_face`: distinct local point numbers, none in upper_face of the same partition; slot s of partition p's lower_face and slot s of partition p-1's upper_face are one shared point. `upper_face`: distinct local point numbers, none in lower_face of the same partition. `step_scale`: Positive.
All inputs are finite; a program needn't handle non-finite values.
Results may differ from the reference program's by a relative error of at most 0.0001.
Values sent between devices are 32-bit elements; how exact they have to be, the bound alone decides.
A program may use at most 64 MiB of HBM per device.

```python
import math
import jax
import jax.numpy as jnp
import numpy as np
from jax import lax

GLL = 5
EX = 4
EY = 4
EZ = 2
RECV_DEV = 128
STEPS = 2
E = 32
NP = 2601
FACE = 289
PARTITIONS = 8
EVENTS = 4
ELEMS = 256
NPTS = 20808
RECV = 1024


def local_numbering(key):
    keys = jax.random.split(key, PARTITIONS)

    def one_partition(single):
        return jax.random.permutation(single, NP)
    return jax.vmap(one_partition)(keys).astype(jnp.int32)


def grid_index():
    node = jnp.arange(GLL * GLL * GLL, dtype=jnp.int32)[:, None]
    elem = jnp.arange(E, dtype=jnp.int32)[None, :]
    width_x = (GLL - 1) * EX + 1
    width_y = (GLL - 1) * EY + 1
    along_x = elem % EX * (GLL - 1) + node % GLL
    along_y = elem // EX % EY * (GLL - 1) + node // GLL % GLL
    along_z = elem // (EX * EY) * (GLL - 1) + node // (GLL * GLL)
    return (along_z * width_y + along_y) * width_x + along_x


def edge_weight(index, count, rim):
    phase = index % 4
    base = jnp.where(phase == 0, 0.2, jnp.where(phase == 2, 32.0 / 45.0, 49.0 / 90.0))
    return jnp.where((index == 0) | (index == count - 1), rim, base).astype(jnp.float32)


def draw_connectivity(key, part):
    numbering = local_numbering(key)
    picked = numbering[:, grid_index()]
    return picked.transpose(1, 0, 2).reshape(GLL * GLL * GLL, PARTITIONS * E).astype(jnp.int32)


def draw_lower_face(key, part):
    numbering = local_numbering(key)
    return numbering[:, :FACE].astype(jnp.int32)


def draw_upper_face(key, part):
    numbering = local_numbering(key)
    return numbering[:, NP - FACE:].astype(jnp.int32)


def draw_step_scale(key, part):
    numbering = local_numbering(key)
    key = jax.random.fold_in(key, 7)
    width_x = (GLL - 1) * EX + 1
    width_y = (GLL - 1) * EY + 1
    width_z = (GLL - 1) * EZ + 1
    position = jnp.arange(NP, dtype=jnp.int32)
    index_x = position % width_x
    index_y = position // width_x % width_y
    index_z = position // (width_x * width_y)
    weight = edge_weight(index_x, width_x, 0.1) * edge_weight(index_y, width_y, 0.1) * edge_weight(index_z, width_z, 0.2)
    spread = jnp.exp(jax.random.uniform(key, (PARTITIONS, NP), jnp.float32, math.log(0.5), math.log(2.0)))
    scale_grid = 0.005 * spread / weight[None, :]
    rows = jnp.arange(PARTITIONS, dtype=jnp.int32)[:, None]
    placed = jnp.zeros((PARTITIONS, NP), jnp.float32).at[rows, numbering].set(scale_grid)
    return placed.reshape(PARTITIONS * NP)


def place_ends(result, key, low, largest):
    dims = result.shape
    place = [jax.random.randint(jax.random.fold_in(key, axis), (), 0, dims[axis]) for axis in range(len(dims))]
    result = result.at[tuple(place)].set(low)
    longest = dims.index(max(dims))
    place[longest] = (place[longest] + 1) % dims[longest]
    return result.at[tuple(place)].set(largest)


def block_levels(key, shape, shards, low, largest):
    gain = 1.0
    for dim, shards_of in shards:
        heights = jax.random.uniform(jax.random.fold_in(jax.random.fold_in(key, 6), dim), (shards_of,), jnp.float32, low / len(shards), largest / len(shards))
        gain = gain * jnp.repeat(jnp.exp(heights), shape[dim] // shards_of).reshape((-1,) + (1,) * (len(shape) - 1 - dim))
    return gain


def centred(key, extent, width, limit, cuts=(), kind=jnp.bfloat16):
    values = width * jax.random.normal(key, extent, jnp.float32)
    if cuts:
        values = values * block_levels(key, extent, cuts, -0.22, 0.18)
    return jnp.clip(values, -limit, limit).astype(kind)


def setup_inputs(seed: int = 0) -> dict:
    arg_keys = jax.random.split(jax.random.key(seed), 13)
    forward_now = centred(arg_keys[0], (EVENTS, 3, NPTS), 1.0, 6.0, ((0, 4), (2, 8)), jnp.float32)
    forward_prev = centred(arg_keys[1], (EVENTS, 3, NPTS), 1.0, 6.0, ((0, 4), (2, 8)), jnp.float32)
    adjoint_now = centred(arg_keys[2], (EVENTS, 3, NPTS), 1.0, 6.0, ((0, 4), (2, 8)), jnp.float32)
    adjoint_prev = centred(arg_keys[3], (EVENTS, 3, NPTS), 1.0, 6.0, ((0, 4), (2, 8)), jnp.float32)
    connectivity = draw_connectivity(jax.random.fold_in(arg_keys[12], 71), 0)
    lower_face = draw_lower_face(jax.random.fold_in(arg_keys[12], 71), 0)
    upper_face = draw_upper_face(jax.random.fold_in(arg_keys[12], 71), 0)
    bulk_modulus = jnp.clip(jnp.exp(math.log(2.0) - 1.3862944 * jax.random.uniform(arg_keys[7], (GLL * GLL * GLL, ELEMS), jnp.float32) ** block_levels(arg_keys[7], (GLL * GLL * GLL, ELEMS), ((1, 8),), -0.2, 0.2)), 0.5, 2.0)
    shear_modulus = jnp.clip(jnp.exp(math.log(1.2) - 1.3862944 * jax.random.uniform(arg_keys[8], (GLL * GLL * GLL, ELEMS), jnp.float32) ** block_levels(arg_keys[8], (GLL * GLL * GLL, ELEMS), ((1, 8),), -0.2, 0.2)), 0.3, 1.2)
    step_scale = draw_step_scale(jax.random.fold_in(arg_keys[12], 71), 0)
    receiver_points = place_ends(jax.random.randint(arg_keys[10], (RECV,), 0, NP), jax.random.fold_in(arg_keys[10], 1), 0, NP - 1).astype(jnp.int32)
    adjoint_source = centred(arg_keys[11], (EVENTS, STEPS, 3, RECV), 3.0, 18.0, ((0, 4), (3, 8)), jnp.float32)
    return {"forward_now": forward_now, "forward_prev": forward_prev, "adjoint_now": adjoint_now, "adjoint_prev": adjoint_prev, "connectivity": connectivity, "lower_face": lower_face, "upper_face": upper_face, "bulk_modulus": bulk_modulus, "shear_modulus": shear_modulus, "step_scale": step_scale, "receiver_points": receiver_points, "adjoint_source": adjoint_source}


kernel_weight = 0.02

def derivative_table():
    root = math.sqrt(3.0 / 7.0)
    points = [-1.0, -root, 0.0, root, 1.0]
    legendre = [(35.0 * x ** 4 - 30.0 * x ** 2 + 3.0) / 8.0 for x in points]
    table = np.zeros((5, 5))
    for row in range(5):
        for column in range(5):
            if row != column:
                table[row, column] = legendre[row] / legendre[column] / (points[row] - points[column])
    table[0, 0] = -2.5
    table[4, 4] = 2.5
    return table

def cube_weights():
    line = np.array([0.1, 49.0 / 90.0, 32.0 / 45.0, 49.0 / 90.0, 0.1])
    cube = line[:, None, None] * line[None, :, None] * line[None, None, :]
    return cube.reshape(125, 1)

def element_terms(values, kappa, shear_mod, deriv, quad):
    count = values.shape[-1]
    top = lax.Precision.HIGHEST
    cube = values.reshape(2, 3, 5, 5, 5, count)
    grad_x = jnp.einsum('ap,fjcbpe->fjcbae', deriv, cube, precision=top)
    grad_y = jnp.einsum('bp,fjcpae->fjcbae', deriv, cube, precision=top)
    grad_z = jnp.einsum('cp,fjpbae->fjcbae', deriv, cube, precision=top)
    grads = jnp.stack([grad_x, grad_y, grad_z]).reshape(3, 2, 3, 125, count).transpose(0, 2, 1, 3, 4)
    strain = 0.5 * (grads + grads.transpose(1, 0, 2, 3, 4))
    dilation = strain[0, 0] + strain[1, 1] + strain[2, 2]
    unit = jnp.eye(3, dtype=jnp.float32)[:, :, None, None, None]
    deviator = strain - unit * (dilation / 3.0)
    stress = unit * (kappa * dilation) + 2.0 * shear_mod * deviator
    bulk = -kernel_weight * kappa * dilation[0] * dilation[1]
    shear = -2.0 * kernel_weight * shear_mod * lax.optimization_barrier(jnp.sum(deviator[:, :, 0] * deviator[:, :, 1], axis=(0, 1)))
    weighted = (quad * stress).reshape(3, 3, 2, 5, 5, 5, count)
    back = jnp.einsum('pa,jfcbpe->jfcbae', deriv, weighted[0], precision=top)
    back = back + jnp.einsum('pb,jfcpae->jfcbae', deriv, weighted[1], precision=top)
    back = back + jnp.einsum('pc,jfpbae->jfcbae', deriv, weighted[2], precision=top)
    forces = -back.transpose(1, 0, 2, 3, 4, 5).reshape(2, 3, 125, count)
    return (forces, bulk, shear)

def reference(forward_now, forward_prev, adjoint_now, adjoint_prev, connectivity, lower_face, upper_face, bulk_modulus, shear_modulus, step_scale, receiver_points, adjoint_source):
    deriv = jnp.asarray(derivative_table(), jnp.float32)
    quad = jnp.asarray(cube_weights(), jnp.float32)
    offsets = jnp.arange(ELEMS, dtype=jnp.int32) // E * NP
    nodes = (connectivity + offsets[None, :]).astype(jnp.int32)
    part_start = (jnp.arange(PARTITIONS, dtype=jnp.int32) * NP)[:, None]
    lower_all = (lower_face + part_start).astype(jnp.int32)
    upper_all = (upper_face + part_start).astype(jnp.int32)
    receivers = (receiver_points + jnp.arange(RECV, dtype=jnp.int32) // RECV_DEV * NP).astype(jnp.int32)

    def one_event(totals, inputs):
        fwd_now, fwd_prev, adj_now, adj_prev, sources = inputs
        waves = jnp.stack([fwd_now, adj_now])
        before = jnp.stack([fwd_prev, adj_prev])
        for step in range(STEPS):
            values = waves[:, :, nodes]
            element_force, bulk, shear = element_terms(values, bulk_modulus, shear_modulus, deriv, quad)
            injected = jnp.zeros((3, NPTS), jnp.float32).at[:, receivers].add(sources[step])
            forces = jnp.stack([jnp.zeros_like(injected), injected])
            forces = forces.at[:, :, nodes].add(element_force)
            upward = forces[:, :, upper_all]
            downward = forces[:, :, lower_all]
            blank = jnp.zeros((2, 3, 1, FACE), jnp.float32)
            below = jnp.concatenate([blank, upward[:, :, :-1]], 2)
            above = jnp.concatenate([downward[:, :, 1:], blank], 2)
            forces = forces.at[:, :, lower_all].add(below).at[:, :, upper_all].add(above)
            following = 2.0 * waves - before + step_scale * forces
            before = waves
            waves = following
            totals = totals + jnp.stack([bulk, shear])
        return (totals, (waves[0], waves[1]))
    start = jnp.zeros((2, 125, ELEMS), jnp.float32)
    totals, results = lax.scan(one_event, start, (forward_now, forward_prev, adjoint_now, adjoint_prev, adjoint_source))
    return (results[0], results[1], totals)
```

```python
import functools
import math

import jax
import jax.numpy as jnp
import numpy as np
from jax import lax
from jax.experimental import pallas as pl
from jax.experimental.pallas import tpu as pltpu
from jax.sharding import PartitionSpec as P

STEPS = 2
LANES = 128
WIDE = 256
KERNEL_WEIGHT = 0.02
MESH = pl.DeviceIdType.MESH
TOP = lax.Precision.HIGHEST


def derivative_table():
    root = math.sqrt(3.0 / 7.0)
    points = [-1.0, -root, 0.0, root, 1.0]
    legendre = [(35.0 * x**4 - 30.0 * x**2 + 3.0) / 8.0 for x in points]
    table = np.zeros((5, 5))
    for row in range(5):
        for column in range(5):
            if row != column:
                table[row, column] = (
                    legendre[row] / legendre[column] / (points[row] - points[column])
                )
    table[0, 0] = -2.5
    table[4, 4] = 2.5
    return table


def cube_tables():
    deriv = derivative_table()
    line = np.array([0.1, 49.0 / 90.0, 32.0 / 45.0, 49.0 / 90.0, 0.1])
    cube = (line[:, None, None] * line[None, :, None] * line[None, None, :]).reshape(125)
    along = [
        np.kron(np.eye(25), deriv),
        np.kron(np.eye(5), np.kron(deriv, np.eye(5))),
        np.kron(deriv, np.eye(25)),
    ]
    ahead = np.zeros((LANES, 3 * LANES))
    back = np.zeros((3 * LANES, LANES))
    for i in range(3):
        ahead[:125, i * LANES : i * LANES + 125] = along[i].T
        back[i * LANES : i * LANES + 125, :125] = -along[i] * cube[:, None]
    return ahead.astype(np.float32), back.astype(np.float32)


def body(
    n_mesh,
    n_event,
    points,
    face,
    elems,
    fwd_now,
    fwd_prev,
    adj_now,
    adj_prev,
    conn,
    lower,
    upper,
    bulk_mod,
    shear_mod,
    scale,
    receivers,
    source,
    ahead,
    back,
    fwd_out,
    adj_out,
    kern_out,
    waves,
    before,
    scale_all,
    forces,
    packed,
    turned,
    rows,
    columns,
    onehot,
    left,
    stress_buf,
    force_buf,
    face_send,
    face_recv,
    kern_send,
    kern_recv,
    face_ssem,
    face_rsem,
    kern_ssem,
    kern_rsem,
):
    me = lax.axis_index("mesh")
    my_event = lax.axis_index("event")
    following = lax.rem(me + 1, n_mesh)
    previous = lax.rem(me + n_mesh - 1, n_mesh)
    barrier = pltpu.get_barrier_semaphore()
    for other in (following, previous):
        pl.semaphore_signal(
            barrier, inc=1, device_id={"mesh": other, "event": my_event}, device_id_type=MESH
        )
    for hop in range(1, n_event):
        peer = lax.rem(my_event + hop, n_event)
        pl.semaphore_signal(
            barrier, inc=1, device_id={"mesh": me, "event": peer}, device_id_type=MESH
        )

    f32 = jnp.float32
    chunks = -(-points // LANES)
    slabs = waves.shape[1] // WIDE
    face_chunks = face_send.shape[3] // LANES
    part_rows = left.shape[0] // 3
    cols = elems // n_event

    waves[...] = jnp.zeros_like(waves)
    before[...] = jnp.zeros_like(before)
    scale_all[...] = jnp.zeros_like(scale_all)
    waves[0:3, 0:points] = fwd_now[0]
    waves[3:6, 0:points] = adj_now[0]
    before[0:3, 0:points] = fwd_prev[0]
    before[3:6, 0:points] = adj_prev[0]
    scale_all[:, 0:points] = jnp.broadcast_to(scale[...], (8, points))

    packed[...] = jnp.zeros_like(packed)
    packed[0:125, 0:elems] = conn[...].astype(f32)
    packed[0:125, elems : 2 * elems] = bulk_mod[...]
    packed[0:125, 2 * elems : 3 * elems] = shear_mod[...]
    turned[...] = packed[...].T
    kappa = turned[elems : 2 * elems]
    mu = turned[2 * elems : 3 * elems]

    rows[...] = jnp.full(rows.shape, -1, jnp.int32)
    rows[0:1, :] = receivers[...]
    for which, ref in enumerate((lower, upper)):
        for k in range(face_chunks):
            size = min(LANES, face - k * LANES)
            at = 1 + which * face_chunks + k
            rows[at : at + 1, 0:size] = ref[:, k * LANES : k * LANES + size]
    columns[...] = rows[...].astype(f32).T.astype(jnp.int32)

    lane = lax.broadcasted_iota(jnp.int32, (LANES, WIDE), 1)

    def spread(at, column):
        low = column & (WIDE - 1)
        onehot[at * LANES : (at + 1) * LANES, :] = jnp.where(lane == low, 1.0, 0.0).astype(
            jnp.bfloat16
        )

    for e in range(elems):
        spread(e, packed[:, e : e + 1].astype(jnp.int32))
    for k in range(1 + 2 * face_chunks):
        spread(elems + k, columns[:, k : k + 1])

    def lookup(table, index, low, high):
        out = jnp.zeros(index.shape, f32)
        for k in range(chunks):
            got = jnp.take_along_axis(table(k), low, axis=1, mode="promise_in_bounds")
            out = jnp.where(high == k, got, out)
        return out

    def place(at, value, index):
        high = index >> 8
        first = value.astype(jnp.bfloat16).astype(f32)
        rest = value - first
        second = rest.astype(jnp.bfloat16).astype(f32)
        third = rest - second
        for s, part in enumerate((first, second, third)):
            slab = [jnp.where(high == k, part, 0.0) for k in range(part_rows // 8)]
            left[s * part_rows : (s + 1) * part_rows, at * LANES : (at + 1) * LANES] = (
                jnp.concatenate(slab, 0).astype(jnp.bfloat16)
            )

    def deposit(start, stop):
        span = slice(start * LANES, stop * LANES)
        total = jnp.dot(left[:, span], onehot[span, :], preferred_element_type=f32)
        return total[0:part_rows] + total[part_rows : 2 * part_rows] + total[2 * part_rows :]

    force_buf[...] = jnp.zeros_like(force_buf)
    bulk = jnp.zeros((elems, LANES), f32)
    shear = jnp.zeros((elems, LANES), f32)
    pending = []
    for step in range(STEPS):
        parts = [[] for _ in range(6)]
        for group in range(elems // 8):
            index = turned[group * 8 : group * 8 + 8, :].astype(jnp.int32)
            low = index & (LANES - 1)
            high = index >> 7
            for c in range(6):
                parts[c].append(
                    lookup(
                        lambda k: jnp.broadcast_to(
                            waves[c : c + 1, k * LANES : (k + 1) * LANES], (8, LANES)
                        ),
                        index,
                        low,
                        high,
                    )
                )
        values = jnp.concatenate([piece for part in parts for piece in part], 0)
        grads = jnp.dot(values, ahead[...], precision=TOP, preferred_element_type=f32)

        def grad(i, c):
            return grads[c * elems : (c + 1) * elems, i * LANES : (i + 1) * LANES]

        divs, devs = [], []
        for f in range(2):
            g = [[grad(i, f * 3 + j) for j in range(3)] for i in range(3)]
            div = g[0][0] + g[1][1] + g[2][2]
            third = div * (1.0 / 3.0)
            dev = {(i, i): g[i][i] - third for i in range(3)}
            for i, j in ((0, 1), (0, 2), (1, 2)):
                dev[i, j] = 0.5 * (g[i][j] + g[j][i])
            divs.append(div)
            devs.append(dev)
            pressure = kappa * div
            for (i, j), term in dev.items():
                tension = 2.0 * mu * term
                if i == j:
                    tension = tension + pressure
                for one, two in {(i, j), (j, i)}:
                    c = f * 3 + two
                    stress_buf[c * elems : (c + 1) * elems, one * LANES : (one + 1) * LANES] = (
                        tension
                    )
        bulk = bulk - KERNEL_WEIGHT * kappa * divs[0] * divs[1]
        both = {key: devs[0][key] * devs[1][key] for key in devs[0]}
        product = both[0, 0] + both[1, 1] + both[2, 2]
        product = product + 2.0 * (both[0, 1] + both[0, 2] + both[1, 2])
        shear = shear - 2.0 * KERNEL_WEIGHT * mu * product

        force_buf[0 : 6 * elems, :] = jnp.dot(
            stress_buf[...], back[...], precision=TOP, preferred_element_type=f32
        )
        for e in range(elems):
            place(
                e,
                force_buf[pl.ds(e, 8, stride=elems), :],
                turned[e : e + 1, :].astype(jnp.int32),
            )
        injected = jnp.concatenate(
            [jnp.zeros((3, LANES), f32), source[0, step], jnp.zeros((2, LANES), f32)], 0
        )
        place(elems, injected, rows[0:1, :])
        total = deposit(0, elems + 1)
        for k in range(slabs):
            forces[:, k * WIDE : (k + 1) * WIDE] = total[8 * k : 8 * k + 8]

        for which in range(2):
            for k in range(face_chunks):
                at = 1 + which * face_chunks + k
                index = jnp.broadcast_to(rows[at : at + 1, :], (8, LANES))
                face_send[step, which, :, k * LANES : (k + 1) * LANES] = lookup(
                    lambda q: forces[:, q * LANES : (q + 1) * LANES],
                    index,
                    index & (LANES - 1),
                    index >> 7,
                )
        if step == 0:
            pl.semaphore_wait(barrier, 2 + n_event - 1)
        copies = []
        for which, other in ((0, previous), (1, following)):
            copy = pltpu.make_async_remote_copy(
                src_ref=face_send.at[step, which],
                dst_ref=face_recv.at[step, 1 - which],
                send_sem=face_ssem.at[step, which],
                recv_sem=face_rsem.at[step, 1 - which],
                device_id={"mesh": other, "event": my_event},
                device_id_type=MESH,
            )
            copy.start()
            copies.append(copy)

        if step == STEPS - 1:
            for owner in range(n_event):
                kern_send[owner, 0] = bulk[owner * cols : (owner + 1) * cols]
                kern_send[owner, 1] = shear[owner * cols : (owner + 1) * cols]
            for hop in range(1, n_event):
                peer = lax.rem(my_event + hop, n_event)
                copy = pltpu.make_async_remote_copy(
                    src_ref=kern_send.at[peer],
                    dst_ref=kern_recv.at[hop - 1],
                    send_sem=kern_ssem.at[hop - 1],
                    recv_sem=kern_rsem.at[hop - 1],
                    device_id={"mesh": me, "event": peer},
                    device_id_type=MESH,
                )
                copy.start()
                pending.append(copy)

        for copy in copies:
            copy.wait()
        for which, inside in ((0, me > 0), (1, me < n_mesh - 1)):
            for k in range(face_chunks):
                at = 1 + which * face_chunks + k
                arrived = face_recv[step, which, :, k * LANES : (k + 1) * LANES]
                arrived = jnp.where(inside, arrived, 0.0)
                place(elems + at, arrived, rows[at : at + 1, :])
        total = deposit(elems + 1, elems + 1 + 2 * face_chunks)
        for k in range(slabs):
            span = slice(k * WIDE, (k + 1) * WIDE)
            assembled = forces[:, span] + total[8 * k : 8 * k + 8]
            now = waves[:, span]
            later = 2.0 * now - before[:, span] + scale_all[:, span] * assembled
            before[:, span] = now
            waves[:, span] = later

    fwd_out[0] = waves[0:3, 0:points]
    adj_out[0] = waves[3:6, 0:points]
    owned = kern_send[my_event]
    for copy in pending:
        copy.wait()
    for hop in range(1, n_event):
        owned = owned + kern_recv[hop - 1]
    for kind in range(2):
        block = jnp.concatenate(
            [owned[kind], jnp.zeros((LANES - cols, LANES), f32)], 0
        )
        kern_out[kind] = block.T[0:125, 0:cols]


def shards(
    n_mesh,
    n_event,
    forward_now,
    forward_prev,
    adjoint_now,
    adjoint_prev,
    connectivity,
    lower_face,
    upper_face,
    bulk_modulus,
    shear_modulus,
    step_scale,
    receiver_points,
    adjoint_source,
):
    points = forward_now.shape[2]
    face = lower_face.shape[1]
    elems = connectivity.shape[1]
    cols = elems // n_event
    slabs = -(-points // WIDE)
    slabs += slabs % 2
    width = slabs * WIDE
    face_chunks = -(-face // LANES)
    blocks = elems + 1 + 2 * face_chunks
    f32 = jnp.float32
    ahead, back = cube_tables()
    vmem = pl.BlockSpec(memory_space=pltpu.VMEM)
    call = pl.pallas_call(
        functools.partial(body, n_mesh, n_event, points, face, elems),
        out_shape=(
            jax.ShapeDtypeStruct(forward_now.shape, f32),
            jax.ShapeDtypeStruct(adjoint_now.shape, f32),
            jax.ShapeDtypeStruct((2, 125, cols), f32),
        ),
        in_specs=[vmem] * 14,
        out_specs=[vmem] * 3,
        scratch_shapes=[
            pltpu.VMEM((8, width), f32),
            pltpu.VMEM((8, width), f32),
            pltpu.VMEM((8, width), f32),
            pltpu.VMEM((8, width), f32),
            pltpu.VMEM((LANES, LANES), f32),
            pltpu.VMEM((LANES, LANES), f32),
            pltpu.VMEM((LANES, LANES), jnp.int32),
            pltpu.VMEM((LANES, LANES), jnp.int32),
            pltpu.VMEM((blocks * LANES, WIDE), jnp.bfloat16),
            pltpu.VMEM((3 * slabs * 8, blocks * LANES), jnp.bfloat16),
            pltpu.VMEM((6 * elems, 3 * LANES), f32),
            pltpu.VMEM((8 * elems, LANES), f32),
            pltpu.VMEM((STEPS, 2, 8, face_chunks * LANES), f32),
            pltpu.VMEM((STEPS, 2, 8, face_chunks * LANES), f32),
            pltpu.VMEM((n_event, 2, cols, LANES), f32),
            pltpu.VMEM((max(n_event - 1, 1), 2, cols, LANES), f32),
            pltpu.SemaphoreType.DMA((STEPS, 2)),
            pltpu.SemaphoreType.DMA((STEPS, 2)),
            pltpu.SemaphoreType.DMA((max(n_event - 1, 1),)),
            pltpu.SemaphoreType.DMA((max(n_event - 1, 1),)),
        ],
        compiler_params=pltpu.CompilerParams(
            collective_id=0, has_side_effects=True, vmem_limit_bytes=48 * 1024 * 1024
        ),
    )
    return call(
        forward_now,
        forward_prev,
        adjoint_now,
        adjoint_prev,
        connectivity,
        lower_face,
        upper_face,
        bulk_modulus,
        shear_modulus,
        step_scale.reshape(1, -1),
        receiver_points.reshape(1, -1),
        adjoint_source,
        jnp.asarray(ahead),
        jnp.asarray(back),
    )


def solution(mesh):
    placed = (
        P("event", None, "mesh"),
        P("event", None, "mesh"),
        P("event", None, "mesh"),
        P("event", None, "mesh"),
        P(None, "mesh"),
        P("mesh", None),
        P("mesh", None),
        P(None, "mesh"),
        P(None, "mesh"),
        P("mesh"),
        P("mesh"),
        P("event", None, None, "mesh"),
    )
    return jax.shard_map(
        functools.partial(shards, mesh.shape["mesh"], mesh.shape["event"]),
        mesh=mesh,
        in_specs=placed,
        out_specs=(
            P("event", None, "mesh"),
            P("event", None, "mesh"),
            P(None, None, ("mesh", "event")),
        ),
        check_vma=False,
    )
```

```python
import functools
import math

import jax
import jax.numpy as jnp
import numpy as np
from jax import lax
from jax.experimental import pallas as pl
from jax.experimental.pallas import tpu as pltpu
from jax.sharding import PartitionSpec as P

STEPS = 2
LANES = 128
WIDE = 256
KERNEL_WEIGHT = 0.02
MESH = pl.DeviceIdType.MESH


def derivative_table():
    root = math.sqrt(3.0 / 7.0)
    points = [-1.0, -root, 0.0, root, 1.0]
    legendre = [(35.0 * x**4 - 30.0 * x**2 + 3.0) / 8.0 for x in points]
    table = np.zeros((5, 5))
    for row in range(5):
        for column in range(5):
            if row != column:
                table[row, column] = (
                    legendre[row] / legendre[column] / (points[row] - points[column])
                )
    table[0, 0] = -2.5
    table[4, 4] = 2.5
    return table


def cube_tables():
    deriv = derivative_table()
    line = np.array([0.1, 49.0 / 90.0, 32.0 / 45.0, 49.0 / 90.0, 0.1])
    cube = (line[:, None, None] * line[None, :, None] * line[None, None, :]).reshape(125)
    along = [
        np.kron(np.eye(25), deriv),
        np.kron(np.eye(5), np.kron(deriv, np.eye(5))),
        np.kron(deriv, np.eye(25)),
    ]
    ahead = np.zeros((LANES, 3 * LANES))
    back = np.zeros((3 * LANES, LANES))
    for i in range(3):
        ahead[:125, i * LANES : i * LANES + 125] = along[i].T
        back[i * LANES : i * LANES + 125, :125] = -along[i] * cube[:, None]
    return stacked(ahead), stacked(back)


def stacked(table):
    rest = table.astype(np.float32)
    parts = []
    for _ in range(3):
        part = rest.astype(jnp.bfloat16)
        rest = rest - part.astype(np.float32)
        parts.append(part)
    first, second, third = parts
    return np.concatenate([first, first, second, second, first, third], 0)


def three_parts(value):
    first = value.astype(jnp.bfloat16)
    rest = value - first.astype(jnp.float32)
    second = rest.astype(jnp.bfloat16)
    third = (rest - second.astype(jnp.float32)).astype(jnp.bfloat16)
    return first, second, third


def product(value, table):
    first, second, third = three_parts(value)
    wide = jnp.concatenate([first, second, first, second, third, first], 1)
    return jnp.dot(wide, table, preferred_element_type=jnp.float32)


def body(n_mesh, n_event, points, face, elems, *refs):
    sources, refs = refs[:14], refs[14:]
    (fwd_out, adj_out, kern_out), refs = refs[:3], refs[3:]
    held, refs = refs[:14], refs[14:]
    (
        fwd_now,
        fwd_prev,
        adj_now,
        adj_prev,
        conn,
        lower,
        upper,
        bulk_mod,
        shear_mod,
        scale,
        receivers,
        source,
        ahead,
        back,
    ) = held
    (
        load_sem,
        waves,
        before,
        later,
        scale_all,
        forces,
        slots,
        kappa_buf,
        mu_buf,
        rows,
        onehot,
        left,
        stress_buf,
        force_buf,
        face_send,
        face_recv,
        kern_send,
        kern_recv,
        face_ssem,
        face_rsem,
        kern_ssem,
        kern_rsem,
    ) = refs
    loads = [
        pltpu.make_async_copy(src, dst, load_sem.at[i])
        for i, (src, dst) in enumerate(zip(sources, held))
    ]
    for i in (4, 5, 6, 10, 0, 2, 12, 7, 8, 13, 11, 1, 3, 9):
        loads[i].start()

    me = lax.axis_index("mesh")
    my_event = lax.axis_index("event")
    following = lax.rem(me + 1, n_mesh)
    previous = lax.rem(me + n_mesh - 1, n_mesh)
    barrier = pltpu.get_barrier_semaphore()
    for other in (following, previous):
        pl.semaphore_signal(
            barrier, inc=1, device_id={"mesh": other, "event": my_event}, device_id_type=MESH
        )
    for hop in range(1, n_event):
        peer = lax.rem(my_event + hop, n_event)
        pl.semaphore_signal(
            barrier, inc=1, device_id={"mesh": me, "event": peer}, device_id_type=MESH
        )

    f32 = jnp.float32
    bf16 = jnp.bfloat16
    chunks = -(-points // LANES)
    slabs = waves.shape[1] // WIDE
    face_chunks = face_send.shape[3] // LANES
    part_rows = left.shape[0] // 3
    cols = elems // n_event
    tile = (8, LANES)

    def lanes_of(k):
        return slice(k * LANES, (k + 1) * LANES)

    rows[...] = jnp.full(rows.shape, -1, jnp.int32)
    waves[...] = jnp.zeros_like(waves)
    before[...] = jnp.zeros_like(before)
    scale_all[...] = jnp.zeros_like(scale_all)
    kappa_buf[...] = jnp.zeros_like(kappa_buf)
    mu_buf[...] = jnp.zeros_like(mu_buf)
    force_buf[...] = jnp.zeros_like(force_buf)
    for i in (4, 5, 6, 10):
        loads[i].wait()
    rows[0:elems, 0:125] = conn[...]
    rows[elems : elems + 1, :] = receivers[...]
    for which, ref in enumerate((lower, upper)):
        for k in range(face_chunks):
            size = min(LANES, face - k * LANES)
            at = elems + 1 + which * face_chunks + k
            rows[at : at + 1, 0:size] = ref[:, k * LANES : k * LANES + size]
    columns = (rows[...].astype(f32).T.astype(jnp.int32) & (WIDE - 1)).astype(f32).astype(bf16)

    lane = lax.broadcasted_iota(jnp.int32, (LANES, WIDE), 1).astype(f32).astype(bf16)
    one = jnp.ones((LANES, WIDE), bf16)
    none = jnp.zeros((LANES, WIDE), bf16)
    half = lax.broadcasted_iota(jnp.int32, (16, LANES), 0) >> 3
    empty = jnp.zeros((16, LANES), bf16)

    def spread(at):
        low = jnp.broadcast_to(columns[:, at : at + 1], (LANES, WIDE))
        onehot[at * LANES : (at + 1) * LANES, :] = jnp.where(lane == low, one, none)

    def take(table, low):
        return jnp.take_along_axis(table, low, axis=1, mode="promise_in_bounds")

    def lookup(tables, index, count):
        low = index & (LANES - 1)
        high = index >> 7
        outs = [jnp.zeros(index.shape, f32) for _ in tables]
        for k in range(count):
            here = high == k
            for t, table in enumerate(tables):
                outs[t] = jnp.where(here, take(table(k), low), outs[t])
        return outs

    def row_of(ref, c):
        return lambda k: jnp.broadcast_to(ref[c : c + 1, lanes_of(k)], tile)

    def place(at, value):
        high = jnp.broadcast_to(rows[at : at + 1, :] >> 8, (16, LANES)) - half
        high = high.astype(f32).astype(bf16)
        parts = three_parts(jnp.concatenate([value, value], 0))
        for k in range(part_rows // 16):
            here = high == jnp.full((16, LANES), 2 * k, bf16)
            for s, part in enumerate(parts):
                row = s * part_rows + 16 * k
                left[row : row + 16, lanes_of(at)] = jnp.where(here, part, empty)

    def deposit(start, stop, out):
        span = slice(start * LANES, stop * LANES)
        total = jnp.dot(left[:, span], onehot[span, :], preferred_element_type=f32)
        total = total[0:part_rows] + total[part_rows : 2 * part_rows] + total[2 * part_rows :]
        for k in range(slabs):
            out[:, k * WIDE : (k + 1) * WIDE] = total[8 * k : 8 * k + 8]

    def element_index(group):
        return rows[group * 8 : group * 8 + 8, :]

    def at_elements(ref):
        parts = [[] for _ in range(6)]
        for group in range(elems // 8):
            got = lookup([row_of(ref, c) for c in range(6)], element_index(group), chunks)
            for c in range(6):
                parts[c].append(got[c])
        return parts

    for i in (0, 2):
        loads[i].wait()
    for c in range(3):
        waves[c : c + 1, 0:points] = fwd_now[c]
        waves[3 + c : 4 + c, 0:points] = adj_now[c]
    parts = at_elements(waves)
    for e in range(elems + 1):
        spread(e)
    for i in (12, 7, 8):
        loads[i].wait()
    kappa_buf[:, 0:125] = bulk_mod[...]
    mu_buf[:, 0:125] = shear_mod[...]
    kappa = kappa_buf[...]
    mu = mu_buf[...]

    span = ahead.shape[0] // 3
    forward_table = jnp.concatenate([ahead[i * span : (i + 1) * span, :] for i in range(3)], 1)
    bulk = jnp.zeros((elems, LANES), f32)
    shear = jnp.zeros((elems, LANES), f32)
    pending = []
    for step in range(STEPS):
        values = jnp.concatenate([piece for part in parts for piece in part], 0)
        grads = product(values, forward_table)

        def grad(i, c):
            return grads[c * elems : (c + 1) * elems, i * LANES : (i + 1) * LANES]

        divs, devs = [], []
        for f in range(2):
            g = [[grad(i, f * 3 + j) for j in range(3)] for i in range(3)]
            div = g[0][0] + g[1][1] + g[2][2]
            third = div * (1.0 / 3.0)
            dev = {(i, i): g[i][i] - third for i in range(3)}
            for i, j in ((0, 1), (0, 2), (1, 2)):
                dev[i, j] = 0.5 * (g[i][j] + g[j][i])
            divs.append(div)
            devs.append(dev)
            pressure = kappa * div
            for (i, j), term in dev.items():
                tension = 2.0 * mu * term
                if i == j:
                    tension = tension + pressure
                for first, second in ((i, j), (j, i))[: 1 + (i != j)]:
                    c = f * 3 + second
                    stress_buf[c * elems : (c + 1) * elems, lanes_of(first)] = tension

        if step == 0:
            loads[13].wait()
        force_buf[0 : 6 * elems, :] = product(stress_buf[...], back[...])
        for e in range(elems):
            place(e, force_buf[pl.ds(e, 8, stride=elems), :])
        if step == 0:
            loads[11].wait()
        injected = jnp.concatenate(
            [jnp.zeros((3, LANES), f32), source[0, :, step, :], jnp.zeros((2, LANES), f32)], 0
        )
        place(elems, injected)
        deposit(0, elems + 1, forces)

        copies = []
        if step == 0:
            pl.semaphore_wait(barrier, 2 + n_event - 1)
        for which, other in ((0, previous), (1, following)):
            for k in range(face_chunks):
                at = elems + 1 + which * face_chunks + k
                index = jnp.broadcast_to(rows[at : at + 1, :], tile)
                face_send[step, which, :, lanes_of(k)] = lookup(
                    [lambda q: forces[:, lanes_of(q)]], index, chunks
                )[0]
            copy = pltpu.make_async_remote_copy(
                src_ref=face_send.at[step, which],
                dst_ref=face_recv.at[step, 1 - which],
                send_sem=face_ssem.at[step, which],
                recv_sem=face_rsem.at[step, 1 - which],
                device_id={"mesh": other, "event": my_event},
                device_id_type=MESH,
            )
            copy.start()
            copies.append(copy)

        bulk = bulk - KERNEL_WEIGHT * kappa * divs[0] * divs[1]
        both = {key: devs[0][key] * devs[1][key] for key in devs[0]}
        paired = both[0, 0] + both[1, 1] + both[2, 2]
        paired = paired + 2.0 * (both[0, 1] + both[0, 2] + both[1, 2])
        shear = shear - 2.0 * KERNEL_WEIGHT * mu * paired

        if step == STEPS - 1:
            for owner in range(n_event):
                kern_send[owner, 0] = bulk[owner * cols : (owner + 1) * cols]
                kern_send[owner, 1] = shear[owner * cols : (owner + 1) * cols]
            for hop in range(1, n_event):
                peer = lax.rem(my_event + hop, n_event)
                copy = pltpu.make_async_remote_copy(
                    src_ref=kern_send.at[peer],
                    dst_ref=kern_recv.at[hop - 1],
                    send_sem=kern_ssem.at[hop - 1],
                    recv_sem=kern_rsem.at[hop - 1],
                    device_id={"mesh": me, "event": peer},
                    device_id_type=MESH,
                )
                copy.start()
                pending.append(copy)

        if step == 0:
            for i in (1, 3, 9):
                loads[i].wait()
            for c in range(3):
                before[c : c + 1, 0:points] = fwd_prev[c]
                before[3 + c : 4 + c, 0:points] = adj_prev[c]
            scale_all[:, 0:points] = jnp.broadcast_to(scale[...].reshape(1, points), (8, points))
            later[...] = 2.0 * waves[...] - before[...] + scale_all[...] * forces[...]
            parts = at_elements(later)
            number = lax.broadcasted_iota(jnp.int32, tile, 1)
            for which, inside in ((0, me > 0), (1, me < n_mesh - 1)):
                for k in range(face_chunks):
                    at = elems + 1 + which * face_chunks + k
                    spread(at)
                    slot = number + ((which * face_chunks + k) * LANES + 1)
                    place(at, jnp.where(inside, slot.astype(f32), 0.0))
            deposit(elems + 1, elems + 1 + 2 * face_chunks, slots)
            extras = [
                lookup([row_of(scale_all, 0), row_of(slots, 0)], element_index(group), chunks)
                for group in range(elems // 8)
            ]
            for copy in copies:
                copy.wait()
            for group in range(elems // 8):
                which = 0 if group < elems // 16 else 1
                factor, slot = extras[group]
                index = slot.astype(jnp.int32) - (1 + which * face_chunks * LANES)
                got = lookup(
                    [row_of(face_recv.at[step, which], c) for c in range(6)], index, face_chunks
                )
                for c in range(6):
                    parts[c][group] = parts[c][group] + factor * got[c]
        else:

            def arrived(at, q):
                index = slots[:, lanes_of(q)].astype(jnp.int32) - 1
                return lookup(
                    [
                        lambda k: face_recv[
                            at, k // face_chunks, :, lanes_of(k % face_chunks)
                        ]
                    ],
                    index,
                    2 * face_chunks,
                )[0]

            for q in range(chunks):
                span = lanes_of(q)
                now = later[:, span] + scale_all[:, span] * arrived(0, q)
                before[:, span] = (
                    2.0 * now - waves[:, span] + scale_all[:, span] * forces[:, span]
                )
            for copy in copies:
                copy.wait()
            for q in range(chunks):
                span = lanes_of(q)
                later[:, span] = before[:, span] + scale_all[:, span] * arrived(1, q)

    for c in range(3):
        fwd_out[c] = later[c : c + 1, 0:points]
        adj_out[c] = later[3 + c : 4 + c, 0:points]
    owned = kern_send[my_event]
    for copy in pending:
        copy.wait()
    for hop in range(1, n_event):
        owned = owned + kern_recv[hop - 1]
    kern_out[...] = owned[:, :, 0:125]


def shards(
    n_mesh,
    n_event,
    forward_now,
    forward_prev,
    adjoint_now,
    adjoint_prev,
    connectivity,
    lower_face,
    upper_face,
    bulk_modulus,
    shear_modulus,
    step_scale,
    receiver_points,
    adjoint_source,
):
    points = forward_now.shape[2]
    face = lower_face.shape[1]
    elems = connectivity.shape[1]
    cols = elems // n_event
    slabs = -(-points // WIDE)
    slabs += slabs % 2
    width = slabs * WIDE
    face_chunks = -(-face // LANES)
    blocks = elems + 1 + 2 * face_chunks
    f32 = jnp.float32
    ahead, back = cube_tables()
    fields = [v.transpose(1, 0, 2) for v in (forward_now, forward_prev, adjoint_now, adjoint_prev)]
    operands = (
        *fields,
        connectivity.T,
        lower_face,
        upper_face,
        bulk_modulus.T,
        shear_modulus.T,
        step_scale,
        receiver_points.reshape(1, -1),
        adjoint_source.transpose(0, 2, 1, 3),
        jnp.asarray(np.concatenate(np.split(ahead, 3, 1), 0)),
        jnp.asarray(back),
    )
    state = pltpu.VMEM((8, width), f32)
    moduli = pltpu.VMEM((elems, LANES), f32)
    peers = max(n_event - 1, 1)
    call = pl.pallas_call(
        functools.partial(body, n_mesh, n_event, points, face, elems),
        out_shape=(
            jax.ShapeDtypeStruct(fields[0].shape, f32),
            jax.ShapeDtypeStruct(fields[2].shape, f32),
            jax.ShapeDtypeStruct((2, cols, 125), f32),
        ),
        in_specs=[pl.BlockSpec(memory_space=pl.ANY)] * 14,
        out_specs=[pl.BlockSpec(memory_space=pltpu.VMEM)] * 3,
        scratch_shapes=[
            *[pltpu.VMEM(v.shape, v.dtype) for v in operands],
            pltpu.SemaphoreType.DMA((14,)),
            state,
            state,
            state,
            state,
            state,
            state,
            moduli,
            moduli,
            pltpu.VMEM((LANES, LANES), jnp.int32),
            pltpu.VMEM((blocks * LANES, WIDE), jnp.bfloat16),
            pltpu.VMEM((3 * slabs * 8, blocks * LANES), jnp.bfloat16),
            pltpu.VMEM((6 * elems, 3 * LANES), f32),
            pltpu.VMEM((8 * elems, LANES), f32),
            pltpu.VMEM((STEPS, 2, 8, face_chunks * LANES), f32),
            pltpu.VMEM((STEPS, 2, 8, face_chunks * LANES), f32),
            pltpu.VMEM((n_event, 2, cols, LANES), f32),
            pltpu.VMEM((peers, 2, cols, LANES), f32),
            pltpu.SemaphoreType.DMA((STEPS, 2)),
            pltpu.SemaphoreType.DMA((STEPS, 2)),
            pltpu.SemaphoreType.DMA((peers,)),
            pltpu.SemaphoreType.DMA((peers,)),
        ],
        compiler_params=pltpu.CompilerParams(
            collective_id=0, has_side_effects=True, vmem_limit_bytes=63 * 1024 * 1024
        ),
    )
    forward, adjoint, kernels = call(*operands)
    return (forward.transpose(1, 0, 2), adjoint.transpose(1, 0, 2), kernels.transpose(0, 2, 1))


def solution(mesh):
    placed = (
        P("event", None, "mesh"),
        P("event", None, "mesh"),
        P("event", None, "mesh"),
        P("event", None, "mesh"),
        P(None, "mesh"),
        P("mesh", None),
        P("mesh", None),
        P(None, "mesh"),
        P(None, "mesh"),
        P("mesh"),
        P("mesh"),
        P("event", None, None, "mesh"),
    )
    return jax.shard_map(
        functools.partial(shards, mesh.shape["mesh"], mesh.shape["event"]),
        mesh=mesh,
        in_specs=placed,
        out_specs=(
            P("event", None, "mesh"),
            P("event", None, "mesh"),
            P(None, None, ("mesh", "event")),
        ),
        check_vma=False,
    )
```

```python
import functools
import math

import jax
import jax.numpy as jnp
import numpy as np
from jax import lax
from jax.experimental import pallas as pl
from jax.experimental.pallas import tpu as pltpu
from jax.sharding import PartitionSpec as P

STEPS = 2
LANES = 128
WIDE = 256
KERNEL_WEIGHT = 0.02
MESH = pl.DeviceIdType.MESH


def derivative_table():
    root = math.sqrt(3.0 / 7.0)
    points = [-1.0, -root, 0.0, root, 1.0]
    legendre = [(35.0 * x**4 - 30.0 * x**2 + 3.0) / 8.0 for x in points]
    table = np.zeros((5, 5))
    for row in range(5):
        for column in range(5):
            if row != column:
                table[row, column] = (
                    legendre[row] / legendre[column] / (points[row] - points[column])
                )
    table[0, 0] = -2.5
    table[4, 4] = 2.5
    return table


def cube_tables():
    deriv = derivative_table()
    line = np.array([0.1, 49.0 / 90.0, 32.0 / 45.0, 49.0 / 90.0, 0.1])
    cube = (line[:, None, None] * line[None, :, None] * line[None, None, :]).reshape(125)
    along = [
        np.kron(np.eye(25), deriv),
        np.kron(np.eye(5), np.kron(deriv, np.eye(5))),
        np.kron(deriv, np.eye(25)),
    ]
    ahead = np.zeros((LANES, 3 * LANES))
    back = np.zeros((3 * LANES, LANES))
    for i in range(3):
        ahead[:125, i * LANES : i * LANES + 125] = along[i].T
        back[i * LANES : i * LANES + 125, :125] = -along[i] * cube[:, None]
    return stacked(ahead), stacked(back)


def stacked(table):
    rest = table.astype(np.float32)
    parts = []
    for _ in range(2):
        part = rest.astype(jnp.bfloat16)
        rest = rest - part.astype(np.float32)
        parts.append(part)
    first, second = parts
    return np.concatenate([first, first, second, second], 0)


def two_parts(value):
    first = value.astype(jnp.bfloat16)
    second = (value - first.astype(jnp.float32)).astype(jnp.bfloat16)
    return first, second


def product(value, table):
    first, second = two_parts(value)
    wide = jnp.concatenate([first, second, first, second], 1)
    return jnp.dot(wide, table, preferred_element_type=jnp.float32)


def body(n_mesh, n_event, points, face, elems, *refs):
    sources, refs = refs[:14], refs[14:]
    (fwd_out, adj_out, kern_out), refs = refs[:3], refs[3:]
    held, refs = refs[:14], refs[14:]
    (
        fwd_now,
        fwd_prev,
        adj_now,
        adj_prev,
        conn,
        lower,
        upper,
        bulk_mod,
        shear_mod,
        scale,
        receivers,
        source,
        ahead,
        back,
    ) = held
    (
        load_sem,
        waves,
        before,
        later,
        scale_all,
        forces,
        slots,
        kappa_buf,
        mu_buf,
        rows,
        onehot,
        left,
        stress_buf,
        force_buf,
        face_send,
        face_recv,
        kern_send,
        kern_recv,
        face_ssem,
        face_rsem,
        kern_ssem,
        kern_rsem,
    ) = refs
    loads = [
        pltpu.make_async_copy(src, dst, load_sem.at[i])
        for i, (src, dst) in enumerate(zip(sources, held))
    ]
    for i in (4, 5, 6, 10, 0, 2, 12, 7, 8, 13, 11, 1, 3, 9):
        loads[i].start()

    me = lax.axis_index("mesh")
    my_event = lax.axis_index("event")
    following = lax.rem(me + 1, n_mesh)
    previous = lax.rem(me + n_mesh - 1, n_mesh)
    barrier = pltpu.get_barrier_semaphore()
    for other in (following, previous):
        pl.semaphore_signal(
            barrier, inc=1, device_id={"mesh": other, "event": my_event}, device_id_type=MESH
        )
    for hop in range(1, n_event):
        peer = lax.rem(my_event + hop, n_event)
        pl.semaphore_signal(
            barrier, inc=1, device_id={"mesh": me, "event": peer}, device_id_type=MESH
        )

    f32 = jnp.float32
    bf16 = jnp.bfloat16
    chunks = -(-points // LANES)
    slabs = waves.shape[1] // WIDE
    face_chunks = face_send.shape[3] // LANES
    part_rows = left.shape[0] // 2
    cols = elems // n_event
    tile = (8, LANES)

    def lanes_of(k):
        return slice(k * LANES, (k + 1) * LANES)

    rows[...] = jnp.full(rows.shape, -1, jnp.int32)
    waves[...] = jnp.zeros_like(waves)
    before[...] = jnp.zeros_like(before)
    scale_all[...] = jnp.zeros_like(scale_all)
    kappa_buf[...] = jnp.zeros_like(kappa_buf)
    mu_buf[...] = jnp.zeros_like(mu_buf)
    force_buf[...] = jnp.zeros_like(force_buf)
    for i in (4, 5, 6, 10):
        loads[i].wait()
    rows[0:elems, 0:125] = conn[...]
    rows[elems : elems + 1, :] = receivers[...]
    for which, ref in enumerate((lower, upper)):
        for k in range(face_chunks):
            size = min(LANES, face - k * LANES)
            at = elems + 1 + which * face_chunks + k
            rows[at : at + 1, 0:size] = ref[:, k * LANES : k * LANES + size]
    columns = (rows[...].astype(f32).T.astype(jnp.int32) & (WIDE - 1)).astype(f32).astype(bf16)

    lane = lax.broadcasted_iota(jnp.int32, (LANES, WIDE), 1).astype(f32).astype(bf16)
    one = jnp.ones((LANES, WIDE), bf16)
    none = jnp.zeros((LANES, WIDE), bf16)
    half = lax.broadcasted_iota(jnp.int32, (16, LANES), 0) >> 3
    empty = jnp.zeros((16, LANES), bf16)

    def spread(at):
        low = jnp.broadcast_to(columns[:, at : at + 1], (LANES, WIDE))
        onehot[at * LANES : (at + 1) * LANES, :] = jnp.where(lane == low, one, none)

    def take(table, low):
        return jnp.take_along_axis(table, low, axis=1, mode="promise_in_bounds")

    def lookup(tables, index, count):
        low = index & (LANES - 1)
        high = index >> 7
        outs = [jnp.zeros(index.shape, f32) for _ in tables]
        for k in range(count):
            here = high == k
            for t, table in enumerate(tables):
                outs[t] = jnp.where(here, take(table(k), low), outs[t])
        return outs

    def row_of(ref, c):
        return lambda k: jnp.broadcast_to(ref[c : c + 1, lanes_of(k)], tile)

    def place(at, value):
        high = jnp.broadcast_to(rows[at : at + 1, :] >> 8, (16, LANES)) - half
        high = high.astype(f32).astype(bf16)
        parts = two_parts(jnp.concatenate([value, value], 0))
        for k in range(part_rows // 16):
            here = high == jnp.full((16, LANES), 2 * k, bf16)
            for s, part in enumerate(parts):
                row = s * part_rows + 16 * k
                left[row : row + 16, lanes_of(at)] = jnp.where(here, part, empty)

    def deposit(start, stop, out):
        span = slice(start * LANES, stop * LANES)
        total = jnp.dot(left[:, span], onehot[span, :], preferred_element_type=f32)
        total = total[0:part_rows] + total[part_rows:]
        for k in range(slabs):
            out[:, k * WIDE : (k + 1) * WIDE] = total[8 * k : 8 * k + 8]

    def element_index(group):
        return rows[group * 8 : group * 8 + 8, :]

    def at_elements(ref):
        parts = [[] for _ in range(6)]
        for group in range(elems // 8):
            got = lookup([row_of(ref, c) for c in range(6)], element_index(group), chunks)
            for c in range(6):
                parts[c].append(got[c])
        return parts

    for i in (0, 2):
        loads[i].wait()
    for c in range(3):
        waves[c : c + 1, 0:points] = fwd_now[c]
        waves[3 + c : 4 + c, 0:points] = adj_now[c]
    parts = at_elements(waves)
    for e in range(elems + 1):
        spread(e)
    for i in (12, 7, 8):
        loads[i].wait()
    kappa_buf[:, 0:125] = bulk_mod[...]
    mu_buf[:, 0:125] = shear_mod[...]
    kappa = kappa_buf[...]
    mu = mu_buf[...]

    span = ahead.shape[0] // 3
    forward_table = jnp.concatenate([ahead[i * span : (i + 1) * span, :] for i in range(3)], 1)
    bulk = jnp.zeros((elems, LANES), f32)
    shear = jnp.zeros((elems, LANES), f32)
    pending = []
    for step in range(STEPS):
        values = jnp.concatenate([piece for part in parts for piece in part], 0)
        grads = product(values, forward_table)

        def grad(i, c):
            return grads[c * elems : (c + 1) * elems, i * LANES : (i + 1) * LANES]

        divs, devs = [], []
        for f in range(2):
            g = [[grad(i, f * 3 + j) for j in range(3)] for i in range(3)]
            div = g[0][0] + g[1][1] + g[2][2]
            third = div * (1.0 / 3.0)
            dev = {(i, i): g[i][i] - third for i in range(3)}
            for i, j in ((0, 1), (0, 2), (1, 2)):
                dev[i, j] = 0.5 * (g[i][j] + g[j][i])
            divs.append(div)
            devs.append(dev)
            pressure = kappa * div
            for (i, j), term in dev.items():
                tension = 2.0 * mu * term
                if i == j:
                    tension = tension + pressure
                for first, second in ((i, j), (j, i))[: 1 + (i != j)]:
                    c = f * 3 + second
                    stress_buf[c * elems : (c + 1) * elems, lanes_of(first)] = tension

        if step == 0:
            loads[13].wait()
        force_buf[0 : 6 * elems, :] = product(stress_buf[...], back[...])
        for e in range(elems):
            place(e, force_buf[pl.ds(e, 8, stride=elems), :])
        if step == 0:
            loads[11].wait()
        injected = jnp.concatenate(
            [jnp.zeros((3, LANES), f32), source[0, :, step, :], jnp.zeros((2, LANES), f32)], 0
        )
        place(elems, injected)
        deposit(0, elems + 1, forces)

        copies = []
        if step == 0:
            pl.semaphore_wait(barrier, 2 + n_event - 1)
        for which, other in ((0, previous), (1, following)):
            for k in range(face_chunks):
                at = elems + 1 + which * face_chunks + k
                index = jnp.broadcast_to(rows[at : at + 1, :], tile)
                face_send[step, which, :, lanes_of(k)] = lookup(
                    [lambda q: forces[:, lanes_of(q)]], index, chunks
                )[0]
            copy = pltpu.make_async_remote_copy(
                src_ref=face_send.at[step, which],
                dst_ref=face_recv.at[step, 1 - which],
                send_sem=face_ssem.at[step, which],
                recv_sem=face_rsem.at[step, 1 - which],
                device_id={"mesh": other, "event": my_event},
                device_id_type=MESH,
            )
            copy.start()
            copies.append(copy)

        bulk = bulk - KERNEL_WEIGHT * kappa * divs[0] * divs[1]
        both = {key: devs[0][key] * devs[1][key] for key in devs[0]}
        paired = both[0, 0] + both[1, 1] + both[2, 2]
        paired = paired + 2.0 * (both[0, 1] + both[0, 2] + both[1, 2])
        shear = shear - 2.0 * KERNEL_WEIGHT * mu * paired

        if step == STEPS - 1:
            for owner in range(n_event):
                kern_send[owner, 0] = bulk[owner * cols : (owner + 1) * cols]
                kern_send[owner, 1] = shear[owner * cols : (owner + 1) * cols]
            for hop in range(1, n_event):
                peer = lax.rem(my_event + hop, n_event)
                copy = pltpu.make_async_remote_copy(
                    src_ref=kern_send.at[peer],
                    dst_ref=kern_recv.at[hop - 1],
                    send_sem=kern_ssem.at[hop - 1],
                    recv_sem=kern_rsem.at[hop - 1],
                    device_id={"mesh": me, "event": peer},
                    device_id_type=MESH,
                )
                copy.start()
                pending.append(copy)

        if step == 0:
            for i in (1, 3, 9):
                loads[i].wait()
            for c in range(3):
                before[c : c + 1, 0:points] = fwd_prev[c]
                before[3 + c : 4 + c, 0:points] = adj_prev[c]
            scale_all[:, 0:points] = jnp.broadcast_to(scale[...].reshape(1, points), (8, points))
            later[...] = 2.0 * waves[...] - before[...] + scale_all[...] * forces[...]
            parts = at_elements(later)
            number = lax.broadcasted_iota(jnp.int32, tile, 1)
            for which, inside in ((0, me > 0), (1, me < n_mesh - 1)):
                for k in range(face_chunks):
                    at = elems + 1 + which * face_chunks + k
                    spread(at)
                    slot = number + ((which * face_chunks + k) * LANES + 1)
                    place(at, jnp.where(inside, slot.astype(f32), 0.0))
            deposit(elems + 1, elems + 1 + 2 * face_chunks, slots)
            extras = [
                lookup([row_of(scale_all, 0), row_of(slots, 0)], element_index(group), chunks)
                for group in range(elems // 8)
            ]
            for copy in copies:
                copy.wait()
            for group in range(elems // 8):
                which = 0 if group < elems // 16 else 1
                factor, slot = extras[group]
                index = slot.astype(jnp.int32) - (1 + which * face_chunks * LANES)
                got = lookup(
                    [row_of(face_recv.at[step, which], c) for c in range(6)], index, face_chunks
                )
                for c in range(6):
                    parts[c][group] = parts[c][group] + factor * got[c]
        else:

            def arrived(at, q):
                index = slots[:, lanes_of(q)].astype(jnp.int32) - 1
                return lookup(
                    [
                        lambda k: face_recv[
                            at, k // face_chunks, :, lanes_of(k % face_chunks)
                        ]
                    ],
                    index,
                    2 * face_chunks,
                )[0]

            for q in range(chunks):
                span = lanes_of(q)
                now = later[:, span] + scale_all[:, span] * arrived(0, q)
                before[:, span] = (
                    2.0 * now - waves[:, span] + scale_all[:, span] * forces[:, span]
                )
            for copy in copies:
                copy.wait()
            for q in range(chunks):
                span = lanes_of(q)
                later[:, span] = before[:, span] + scale_all[:, span] * arrived(1, q)

    for c in range(3):
        fwd_out[c] = later[c : c + 1, 0:points]
        adj_out[c] = later[3 + c : 4 + c, 0:points]
    owned = kern_send[my_event]
    for copy in pending:
        copy.wait()
    for hop in range(1, n_event):
        owned = owned + kern_recv[hop - 1]
    kern_out[...] = owned[:, :, 0:125]


def copy_out(*refs):
    count = len(refs) // 2
    sem = refs[-1]
    copies = [pltpu.make_async_copy(refs[i], refs[count + i], sem.at[i]) for i in range(count)]
    for copy in copies:
        copy.start()
    for copy in copies:
        copy.wait()


def hand_out(results):
    count = len(results)
    return pl.pallas_call(
        copy_out,
        out_shape=tuple(jax.ShapeDtypeStruct(v.shape, v.dtype) for v in results),
        in_specs=[pl.BlockSpec(memory_space=pltpu.HBM)] * count,
        out_specs=[pl.BlockSpec(memory_space=pltpu.HBM)] * count,
        scratch_shapes=[pltpu.SemaphoreType.DMA((count,))],
        compiler_params=pltpu.CompilerParams(vmem_limit_bytes=60 * 1024 * 1024),
    )(*results)


def shards(
    n_mesh,
    n_event,
    forward_now,
    forward_prev,
    adjoint_now,
    adjoint_prev,
    connectivity,
    lower_face,
    upper_face,
    bulk_modulus,
    shear_modulus,
    step_scale,
    receiver_points,
    adjoint_source,
):
    points = forward_now.shape[2]
    face = lower_face.shape[1]
    elems = connectivity.shape[1]
    cols = elems // n_event
    slabs = -(-points // WIDE)
    slabs += slabs % 2
    width = slabs * WIDE
    face_chunks = -(-face // LANES)
    blocks = elems + 1 + 2 * face_chunks
    f32 = jnp.float32
    ahead, back = cube_tables()
    fields = [v.transpose(1, 0, 2) for v in (forward_now, forward_prev, adjoint_now, adjoint_prev)]
    operands = (
        *fields,
        connectivity.T,
        lower_face,
        upper_face,
        bulk_modulus.T,
        shear_modulus.T,
        step_scale,
        receiver_points.reshape(1, -1),
        adjoint_source.transpose(0, 2, 1, 3),
        jnp.asarray(np.concatenate(np.split(ahead, 3, 1), 0)),
        jnp.asarray(back),
    )
    state = pltpu.VMEM((8, width), f32)
    moduli = pltpu.VMEM((elems, LANES), f32)
    peers = max(n_event - 1, 1)
    call = pl.pallas_call(
        functools.partial(body, n_mesh, n_event, points, face, elems),
        out_shape=(
            jax.ShapeDtypeStruct(fields[0].shape, f32),
            jax.ShapeDtypeStruct(fields[2].shape, f32),
            jax.ShapeDtypeStruct((2, cols, 125), f32),
        ),
        in_specs=[pl.BlockSpec(memory_space=pltpu.HBM)] * 14,
        out_specs=[pl.BlockSpec(memory_space=pltpu.VMEM)] * 3,
        scratch_shapes=[
            *[pltpu.VMEM(v.shape, v.dtype) for v in operands],
            pltpu.SemaphoreType.DMA((14,)),
            state,
            state,
            state,
            state,
            state,
            state,
            moduli,
            moduli,
            pltpu.VMEM((LANES, LANES), jnp.int32),
            pltpu.VMEM((blocks * LANES, WIDE), jnp.bfloat16),
            pltpu.VMEM((2 * slabs * 8, blocks * LANES), jnp.bfloat16),
            pltpu.VMEM((6 * elems, 3 * LANES), f32),
            pltpu.VMEM((8 * elems, LANES), f32),
            pltpu.VMEM((STEPS, 2, 8, face_chunks * LANES), f32),
            pltpu.VMEM((STEPS, 2, 8, face_chunks * LANES), f32),
            pltpu.VMEM((n_event, 2, cols, LANES), f32),
            pltpu.VMEM((peers, 2, cols, LANES), f32),
            pltpu.SemaphoreType.DMA((STEPS, 2)),
            pltpu.SemaphoreType.DMA((STEPS, 2)),
            pltpu.SemaphoreType.DMA((peers,)),
            pltpu.SemaphoreType.DMA((peers,)),
        ],
        compiler_params=pltpu.CompilerParams(
            collective_id=0, has_side_effects=True, vmem_limit_bytes=60 * 1024 * 1024
        ),
    )
    forward, adjoint, kernels = hand_out(call(*operands))
    return (forward.transpose(1, 0, 2), adjoint.transpose(1, 0, 2), kernels.transpose(0, 2, 1))


def solution(mesh):
    placed = (
        P("event", None, "mesh"),
        P("event", None, "mesh"),
        P("event", None, "mesh"),
        P("event", None, "mesh"),
        P(None, "mesh"),
        P("mesh", None),
        P("mesh", None),
        P(None, "mesh"),
        P(None, "mesh"),
        P("mesh"),
        P("mesh"),
        P("event", None, None, "mesh"),
    )
    return jax.shard_map(
        functools.partial(shards, mesh.shape["mesh"], mesh.shape["event"]),
        mesh=mesh,
        in_specs=placed,
        out_specs=(
            P("event", None, "mesh"),
            P("event", None, "mesh"),
            P(None, None, ("mesh", "event")),
        ),
        check_vma=False,
    )
```

```python
import functools
import math

import jax
import jax.numpy as jnp
import numpy as np
from jax import lax
from jax.experimental import pallas as pl
from jax.experimental.pallas import tpu as pltpu
from jax.sharding import PartitionSpec as P

STEPS = 2
LANES = 128
WIDE = 256
KERNEL_WEIGHT = 0.02
MESH = pl.DeviceIdType.MESH


def derivative_table():
    root = math.sqrt(3.0 / 7.0)
    points = [-1.0, -root, 0.0, root, 1.0]
    legendre = [(35.0 * x**4 - 30.0 * x**2 + 3.0) / 8.0 for x in points]
    table = np.zeros((5, 5))
    for row in range(5):
        for column in range(5):
            if row != column:
                table[row, column] = (
                    legendre[row] / legendre[column] / (points[row] - points[column])
                )
    table[0, 0] = -2.5
    table[4, 4] = 2.5
    return table


def cube_tables():
    deriv = derivative_table()
    line = np.array([0.1, 49.0 / 90.0, 32.0 / 45.0, 49.0 / 90.0, 0.1])
    cube = (line[:, None, None] * line[None, :, None] * line[None, None, :]).reshape(125)
    along = [
        np.kron(np.eye(25), deriv),
        np.kron(np.eye(5), np.kron(deriv, np.eye(5))),
        np.kron(deriv, np.eye(25)),
    ]
    ahead = np.zeros((LANES, 3 * LANES))
    back = np.zeros((3 * LANES, LANES))
    for i in range(3):
        ahead[:125, i * LANES : i * LANES + 125] = along[i].T
        back[i * LANES : i * LANES + 125, :125] = -along[i] * cube[:, None]
    return stacked(ahead), stacked(back)


def stacked(table):
    rest = table.astype(np.float32)
    parts = []
    for _ in range(2):
        part = rest.astype(jnp.bfloat16)
        rest = rest - part.astype(np.float32)
        parts.append(part)
    first, second = parts
    return np.concatenate([first, first, second, second], 0)


def two_parts(value):
    first = value.astype(jnp.bfloat16)
    second = (value - first.astype(jnp.float32)).astype(jnp.bfloat16)
    return first, second


def product(value, table):
    first, second = two_parts(value)
    wide = jnp.concatenate([first, second, first, second], 1)
    return jnp.dot(wide, table, preferred_element_type=jnp.float32)


def body(n_mesh, n_event, points, face, elems, *refs):
    sources, refs = refs[:14], refs[14:]
    (fwd_out, adj_out, kern_out), refs = refs[:3], refs[3:]
    held, refs = refs[:14], refs[14:]
    (
        fwd_now,
        fwd_prev,
        adj_now,
        adj_prev,
        conn,
        lower,
        upper,
        bulk_mod,
        shear_mod,
        scale,
        receivers,
        source,
        ahead,
        back,
    ) = held
    (
        load_sem,
        waves,
        before,
        later,
        scale_all,
        forces,
        slots,
        kappa_buf,
        mu_buf,
        rows,
        onehot,
        left,
        stress_buf,
        force_buf,
        face_send,
        face_recv,
        kern_send,
        kern_recv,
        face_ssem,
        face_rsem,
        kern_ssem,
        kern_rsem,
    ) = refs
    loads = [
        pltpu.make_async_copy(src, dst, load_sem.at[i])
        for i, (src, dst) in enumerate(zip(sources, held))
    ]
    for i in (4, 5, 6, 10, 0, 2, 12, 7, 8, 13, 11, 1, 3, 9):
        loads[i].start()

    me = lax.axis_index("mesh")
    my_event = lax.axis_index("event")
    following = lax.rem(me + 1, n_mesh)
    previous = lax.rem(me + n_mesh - 1, n_mesh)
    barrier = pltpu.get_barrier_semaphore()
    for other in (following, previous):
        pl.semaphore_signal(
            barrier, inc=1, device_id={"mesh": other, "event": my_event}, device_id_type=MESH
        )
    for hop in range(1, n_event):
        peer = lax.rem(my_event + hop, n_event)
        pl.semaphore_signal(
            barrier, inc=1, device_id={"mesh": me, "event": peer}, device_id_type=MESH
        )

    f32 = jnp.float32
    bf16 = jnp.bfloat16
    chunks = -(-points // LANES)
    slabs = waves.shape[1] // WIDE
    face_chunks = face_send.shape[3] // LANES
    part_rows = left.shape[0] // 2
    cols = elems // n_event
    tile = (8, LANES)

    def lanes_of(k):
        return slice(k * LANES, (k + 1) * LANES)

    rows[...] = jnp.full(rows.shape, -1, jnp.int32)
    waves[...] = jnp.zeros_like(waves)
    before[...] = jnp.zeros_like(before)
    scale_all[...] = jnp.zeros_like(scale_all)
    kappa_buf[...] = jnp.zeros_like(kappa_buf)
    mu_buf[...] = jnp.zeros_like(mu_buf)
    force_buf[...] = jnp.zeros_like(force_buf)
    for i in (4, 5, 6, 10):
        loads[i].wait()
    rows[0:elems, 0:125] = conn[...]
    rows[elems : elems + 1, :] = receivers[...]
    for which, ref in enumerate((lower, upper)):
        for k in range(face_chunks):
            size = min(LANES, face - k * LANES)
            at = elems + 1 + which * face_chunks + k
            rows[at : at + 1, 0:size] = ref[:, k * LANES : k * LANES + size]
    columns = (rows[...].astype(f32).T.astype(jnp.int32) & (WIDE - 1)).astype(f32).astype(bf16)

    lane = lax.broadcasted_iota(jnp.int32, (LANES, WIDE), 1).astype(f32).astype(bf16)
    one = jnp.ones((LANES, WIDE), bf16)
    none = jnp.zeros((LANES, WIDE), bf16)
    half = lax.broadcasted_iota(jnp.int32, (16, LANES), 0) >> 3
    empty = jnp.zeros((16, LANES), bf16)

    def spread(at):
        low = jnp.broadcast_to(columns[:, at : at + 1], (LANES, WIDE))
        onehot[at * LANES : (at + 1) * LANES, :] = jnp.where(lane == low, one, none)

    def take(table, low):
        return jnp.take_along_axis(table, low, axis=1, mode="promise_in_bounds")

    def lookup(tables, index, count):
        low = index & (LANES - 1)
        high = index >> 7
        outs = [jnp.zeros(index.shape, f32) for _ in tables]
        for k in range(count):
            here = high == k
            for t, table in enumerate(tables):
                outs[t] = jnp.where(here, take(table(k), low), outs[t])
        return outs

    def row_of(ref, c):
        return lambda k: jnp.broadcast_to(ref[c : c + 1, lanes_of(k)], tile)

    def place(at, value):
        high = jnp.broadcast_to(rows[at : at + 1, :] >> 8, (16, LANES)) - half
        high = high.astype(f32).astype(bf16)
        parts = two_parts(jnp.concatenate([value, value], 0))
        for k in range(part_rows // 16):
            here = high == jnp.full((16, LANES), 2 * k, bf16)
            for s, part in enumerate(parts):
                row = s * part_rows + 16 * k
                left[row : row + 16, lanes_of(at)] = jnp.where(here, part, empty)

    def deposit(start, stop, out):
        span = slice(start * LANES, stop * LANES)
        total = jnp.dot(left[:, span], onehot[span, :], preferred_element_type=f32)
        total = total[0:part_rows] + total[part_rows:]
        for k in range(slabs):
            out[:, k * WIDE : (k + 1) * WIDE] = total[8 * k : 8 * k + 8]

    def element_index(group):
        return rows[group * 8 : group * 8 + 8, :]

    def at_elements(ref):
        parts = [[] for _ in range(6)]
        for group in range(elems // 8):
            got = lookup([row_of(ref, c) for c in range(6)], element_index(group), chunks)
            for c in range(6):
                parts[c].append(got[c])
        return parts

    for i in (0, 2):
        loads[i].wait()
    for c in range(3):
        waves[c : c + 1, 0:points] = fwd_now[c]
        waves[3 + c : 4 + c, 0:points] = adj_now[c]
    parts = at_elements(waves)
    for e in range(elems + 1):
        spread(e)
    for i in (12, 7, 8):
        loads[i].wait()
    kappa_buf[:, 0:125] = bulk_mod[...]
    mu_buf[:, 0:125] = shear_mod[...]
    kappa = kappa_buf[...]
    mu = mu_buf[...]

    span = ahead.shape[0] // 3
    forward_table = jnp.concatenate([ahead[i * span : (i + 1) * span, :] for i in range(3)], 1)
    bulk = jnp.zeros((elems, LANES), f32)
    shear = jnp.zeros((elems, LANES), f32)
    pending = []
    for step in range(STEPS):
        values = jnp.concatenate([piece for part in parts for piece in part], 0)
        grads = product(values, forward_table)

        def grad(i, c):
            return grads[c * elems : (c + 1) * elems, i * LANES : (i + 1) * LANES]

        divs, devs = [], []
        for f in range(2):
            g = [[grad(i, f * 3 + j) for j in range(3)] for i in range(3)]
            div = g[0][0] + g[1][1] + g[2][2]
            third = div * (1.0 / 3.0)
            dev = {(i, i): g[i][i] - third for i in range(3)}
            for i, j in ((0, 1), (0, 2), (1, 2)):
                dev[i, j] = 0.5 * (g[i][j] + g[j][i])
            divs.append(div)
            devs.append(dev)
            pressure = kappa * div
            for (i, j), term in dev.items():
                tension = 2.0 * mu * term
                if i == j:
                    tension = tension + pressure
                for first, second in ((i, j), (j, i))[: 1 + (i != j)]:
                    c = f * 3 + second
                    stress_buf[c * elems : (c + 1) * elems, lanes_of(first)] = tension

        if step == 0:
            loads[13].wait()
        force_buf[0 : 6 * elems, :] = product(stress_buf[...], back[...])
        for e in range(elems):
            place(e, force_buf[pl.ds(e, 8, stride=elems), :])
        if step == 0:
            loads[11].wait()
        injected = jnp.concatenate(
            [jnp.zeros((3, LANES), f32), source[0, :, step, :], jnp.zeros((2, LANES), f32)], 0
        )
        place(elems, injected)
        deposit(0, elems + 1, forces)

        copies = []
        if step == 0:
            pl.semaphore_wait(barrier, 2 + n_event - 1)
        for which, other in ((0, previous), (1, following)):
            for k in range(face_chunks):
                at = elems + 1 + which * face_chunks + k
                index = jnp.broadcast_to(rows[at : at + 1, :], tile)
                face_send[step, which, :, lanes_of(k)] = lookup(
                    [lambda q: forces[:, lanes_of(q)]], index, chunks
                )[0]
            copy = pltpu.make_async_remote_copy(
                src_ref=face_send.at[step, which],
                dst_ref=face_recv.at[step, 1 - which],
                send_sem=face_ssem.at[step, which],
                recv_sem=face_rsem.at[step, 1 - which],
                device_id={"mesh": other, "event": my_event},
                device_id_type=MESH,
            )
            copy.start()
            copies.append(copy)

        bulk = bulk - KERNEL_WEIGHT * kappa * divs[0] * divs[1]
        both = {key: devs[0][key] * devs[1][key] for key in devs[0]}
        paired = both[0, 0] + both[1, 1] + both[2, 2]
        paired = paired + 2.0 * (both[0, 1] + both[0, 2] + both[1, 2])
        shear = shear - 2.0 * KERNEL_WEIGHT * mu * paired

        if step == STEPS - 1:
            for owner in range(n_event):
                kern_send[owner, 0] = bulk[owner * cols : (owner + 1) * cols]
                kern_send[owner, 1] = shear[owner * cols : (owner + 1) * cols]
            for hop in range(1, n_event):
                peer = lax.rem(my_event + hop, n_event)
                copy = pltpu.make_async_remote_copy(
                    src_ref=kern_send.at[peer],
                    dst_ref=kern_recv.at[hop - 1],
                    send_sem=kern_ssem.at[hop - 1],
                    recv_sem=kern_rsem.at[hop - 1],
                    device_id={"mesh": me, "event": peer},
                    device_id_type=MESH,
                )
                copy.start()
                pending.append(copy)

        if step == 0:
            for i in (1, 3, 9):
                loads[i].wait()
            for c in range(3):
                before[c : c + 1, 0:points] = fwd_prev[c]
                before[3 + c : 4 + c, 0:points] = adj_prev[c]
            scale_all[:, 0:points] = jnp.broadcast_to(scale[...].reshape(1, points), (8, points))
            later[...] = 2.0 * waves[...] - before[...] + scale_all[...] * forces[...]
            parts = at_elements(later)
            number = lax.broadcasted_iota(jnp.int32, tile, 1)
            for which, inside in ((0, me > 0), (1, me < n_mesh - 1)):
                for k in range(face_chunks):
                    at = elems + 1 + which * face_chunks + k
                    spread(at)
                    slot = number + ((which * face_chunks + k) * LANES + 1)
                    place(at, jnp.where(inside, slot.astype(f32), 0.0))
            deposit(elems + 1, elems + 1 + 2 * face_chunks, slots)
            extras = [
                lookup([row_of(scale_all, 0), row_of(slots, 0)], element_index(group), chunks)
                for group in range(elems // 8)
            ]
            for copy in copies:
                copy.wait()
            for group in range(elems // 8):
                which = 0 if group < elems // 16 else 1
                factor, slot = extras[group]
                index = slot.astype(jnp.int32) - (1 + which * face_chunks * LANES)
                got = lookup(
                    [row_of(face_recv.at[step, which], c) for c in range(6)], index, face_chunks
                )
                for c in range(6):
                    parts[c][group] = parts[c][group] + factor * got[c]
        else:

            def arrived(at, q):
                index = slots[:, lanes_of(q)].astype(jnp.int32) - 1
                return lookup(
                    [
                        lambda k: face_recv[
                            at, k // face_chunks, :, lanes_of(k % face_chunks)
                        ]
                    ],
                    index,
                    2 * face_chunks,
                )[0]

            for q in range(chunks):
                span = lanes_of(q)
                now = later[:, span] + scale_all[:, span] * arrived(0, q)
                before[:, span] = (
                    2.0 * now - waves[:, span] + scale_all[:, span] * forces[:, span]
                )
            for copy in copies:
                copy.wait()
            for q in range(chunks):
                span = lanes_of(q)
                later[:, span] = before[:, span] + scale_all[:, span] * arrived(1, q)

    for c in range(3):
        fwd_out[c] = later[c : c + 1, 0:points]
        adj_out[c] = later[3 + c : 4 + c, 0:points]
    owned = kern_send[my_event]
    for copy in pending:
        copy.wait()
    for hop in range(1, n_event):
        owned = owned + kern_recv[hop - 1]
    kern_out[...] = owned[:, :, 0:125]


def copy_out(*refs):
    count = len(refs) // 2
    sem = refs[-1]
    copies = [pltpu.make_async_copy(refs[i], refs[count + i], sem.at[i]) for i in range(count)]
    for copy in copies:
        copy.start()
    for copy in copies:
        copy.wait()


def hand_out(results):
    count = len(results)
    return pl.pallas_call(
        copy_out,
        out_shape=tuple(jax.ShapeDtypeStruct(v.shape, v.dtype) for v in results),
        in_specs=[pl.BlockSpec(memory_space=pltpu.VMEM)] * count,
        out_specs=[pl.BlockSpec(memory_space=pltpu.HBM)] * count,
        scratch_shapes=[pltpu.SemaphoreType.DMA((count,))],
        compiler_params=pltpu.CompilerParams(vmem_limit_bytes=1024 * 1024),
    )(*results)


def shards(
    n_mesh,
    n_event,
    forward_now,
    forward_prev,
    adjoint_now,
    adjoint_prev,
    connectivity,
    lower_face,
    upper_face,
    bulk_modulus,
    shear_modulus,
    step_scale,
    receiver_points,
    adjoint_source,
):
    points = forward_now.shape[2]
    face = lower_face.shape[1]
    elems = connectivity.shape[1]
    cols = elems // n_event
    slabs = -(-points // WIDE)
    slabs += slabs % 2
    width = slabs * WIDE
    face_chunks = -(-face // LANES)
    blocks = elems + 1 + 2 * face_chunks
    f32 = jnp.float32
    ahead, back = cube_tables()
    fields = [v.transpose(1, 0, 2) for v in (forward_now, forward_prev, adjoint_now, adjoint_prev)]
    operands = (
        *fields,
        connectivity.T,
        lower_face,
        upper_face,
        bulk_modulus.T,
        shear_modulus.T,
        step_scale,
        receiver_points.reshape(1, -1),
        adjoint_source.transpose(0, 2, 1, 3),
        jnp.asarray(np.concatenate(np.split(ahead, 3, 1), 0)),
        jnp.asarray(back),
    )
    state = pltpu.VMEM((8, width), f32)
    moduli = pltpu.VMEM((elems, LANES), f32)
    peers = max(n_event - 1, 1)
    call = pl.pallas_call(
        functools.partial(body, n_mesh, n_event, points, face, elems),
        out_shape=(
            pltpu.VMEM(fields[0].shape, f32),
            pltpu.VMEM(fields[2].shape, f32),
            pltpu.VMEM((2, cols, 125), f32),
        ),
        in_specs=[pl.BlockSpec(memory_space=pltpu.HBM)] * 14,
        out_specs=[pl.BlockSpec(memory_space=pltpu.VMEM)] * 3,
        scratch_shapes=[
            *[pltpu.VMEM(v.shape, v.dtype) for v in operands],
            pltpu.SemaphoreType.DMA((14,)),
            state,
            state,
            state,
            state,
            state,
            state,
            moduli,
            moduli,
            pltpu.VMEM((LANES, LANES), jnp.int32),
            pltpu.VMEM((blocks * LANES, WIDE), jnp.bfloat16),
            pltpu.VMEM((2 * slabs * 8, blocks * LANES), jnp.bfloat16),
            pltpu.VMEM((6 * elems, 3 * LANES), f32),
            pltpu.VMEM((8 * elems, LANES), f32),
            pltpu.VMEM((STEPS, 2, 8, face_chunks * LANES), f32),
            pltpu.VMEM((STEPS, 2, 8, face_chunks * LANES), f32),
            pltpu.VMEM((n_event, 2, cols, LANES), f32),
            pltpu.VMEM((peers, 2, cols, LANES), f32),
            pltpu.SemaphoreType.DMA((STEPS, 2)),
            pltpu.SemaphoreType.DMA((STEPS, 2)),
            pltpu.SemaphoreType.DMA((peers,)),
            pltpu.SemaphoreType.DMA((peers,)),
        ],
        compiler_params=pltpu.CompilerParams(
            collective_id=0, has_side_effects=True, vmem_limit_bytes=60 * 1024 * 1024
        ),
    )
    forward, adjoint, kernels = hand_out(call(*operands))
    return (forward.transpose(1, 0, 2), adjoint.transpose(1, 0, 2), kernels.transpose(0, 2, 1))


def solution(mesh):
    placed = (
        P("event", None, "mesh"),
        P("event", None, "mesh"),
        P("event", None, "mesh"),
        P("event", None, "mesh"),
        P(None, "mesh"),
        P("mesh", None),
        P("mesh", None),
        P(None, "mesh"),
        P(None, "mesh"),
        P("mesh"),
        P("mesh"),
        P("event", None, None, "mesh"),
    )
    return jax.shard_map(
        functools.partial(shards, mesh.shape["mesh"], mesh.shape["event"]),
        mesh=mesh,
        in_specs=placed,
        out_specs=(
            P("event", None, "mesh"),
            P("event", None, "mesh"),
            P(None, None, ("mesh", "event")),
        ),
        check_vma=False,
    )
```

```python
import functools
import math

import jax
import jax.numpy as jnp
import numpy as np
from jax import lax
from jax.experimental import pallas as pl
from jax.experimental.pallas import tpu as pltpu
from jax.sharding import PartitionSpec as P

STEPS = 2
LANES = 128
WIDE = 256
KERNEL_WEIGHT = 0.02
MESH = pl.DeviceIdType.MESH


def derivative_table():
    root = math.sqrt(3.0 / 7.0)
    points = [-1.0, -root, 0.0, root, 1.0]
    legendre = [(35.0 * x**4 - 30.0 * x**2 + 3.0) / 8.0 for x in points]
    table = np.zeros((5, 5))
    for row in range(5):
        for column in range(5):
            if row != column:
                table[row, column] = (
                    legendre[row] / legendre[column] / (points[row] - points[column])
                )
    table[0, 0] = -2.5
    table[4, 4] = 2.5
    return table


def cube_tables():
    deriv = derivative_table()
    line = np.array([0.1, 49.0 / 90.0, 32.0 / 45.0, 49.0 / 90.0, 0.1])
    cube = (line[:, None, None] * line[None, :, None] * line[None, None, :]).reshape(125)
    along = [
        np.kron(np.eye(25), deriv),
        np.kron(np.eye(5), np.kron(deriv, np.eye(5))),
        np.kron(deriv, np.eye(25)),
    ]
    ahead = np.zeros((LANES, 3 * LANES))
    back = np.zeros((3 * LANES, LANES))
    for i in range(3):
        ahead[:125, i * LANES : i * LANES + 125] = along[i].T
        back[i * LANES : i * LANES + 125, :125] = -along[i] * cube[:, None]
    return stacked(ahead), stacked(back)


def stacked(table):
    rest = table.astype(np.float32)
    parts = []
    for _ in range(2):
        part = rest.astype(jnp.bfloat16)
        rest = rest - part.astype(np.float32)
        parts.append(part)
    first, second = parts
    return np.concatenate([first, first, second], 0)


def two_parts(value):
    first = value.astype(jnp.bfloat16)
    second = (value - first.astype(jnp.float32)).astype(jnp.bfloat16)
    return first, second


def product(value, table):
    first, second = two_parts(value)
    wide = jnp.concatenate([first, second, first], 1)
    return jnp.dot(wide, table, preferred_element_type=jnp.float32)


def body(n_mesh, n_event, points, face, elems, *refs):
    sources, refs = refs[:14], refs[14:]
    (fwd_out, adj_out, kern_out), refs = refs[:3], refs[3:]
    held, refs = refs[:14], refs[14:]
    (
        fwd_now,
        fwd_prev,
        adj_now,
        adj_prev,
        conn,
        lower,
        upper,
        bulk_mod,
        shear_mod,
        scale,
        receivers,
        source,
        ahead,
        back,
    ) = held
    (
        load_sem,
        waves,
        before,
        later,
        scale_all,
        forces,
        slots,
        kappa_buf,
        mu_buf,
        rows,
        onehot,
        left,
        stress_buf,
        force_buf,
        face_send,
        face_recv,
        face_scaled,
        kern_send,
        kern_recv,
        face_ssem,
        face_rsem,
        kern_ssem,
        kern_rsem,
    ) = refs
    loads = [
        pltpu.make_async_copy(src, dst, load_sem.at[i])
        for i, (src, dst) in enumerate(zip(sources, held))
    ]
    for i in (4, 5, 6, 10, 0, 2, 12, 7, 8, 13, 11, 1, 3, 9):
        loads[i].start()

    me = lax.axis_index("mesh")
    my_event = lax.axis_index("event")
    following = lax.rem(me + 1, n_mesh)
    previous = lax.rem(me + n_mesh - 1, n_mesh)
    barrier = pltpu.get_barrier_semaphore()
    for other in (following, previous):
        pl.semaphore_signal(
            barrier, inc=1, device_id={"mesh": other, "event": my_event}, device_id_type=MESH
        )
    for hop in range(1, n_event):
        peer = lax.rem(my_event + hop, n_event)
        pl.semaphore_signal(
            barrier, inc=1, device_id={"mesh": me, "event": peer}, device_id_type=MESH
        )

    f32 = jnp.float32
    bf16 = jnp.bfloat16
    chunks = -(-points // LANES)
    slabs = waves.shape[1] // WIDE
    face_chunks = face_send.shape[3] // LANES
    part_rows = left.shape[0] // 2
    cols = elems // n_event
    tile = (8, LANES)

    def lanes_of(k):
        return slice(k * LANES, (k + 1) * LANES)

    rows[...] = jnp.full(rows.shape, -1, jnp.int32)
    waves[...] = jnp.zeros_like(waves)
    before[...] = jnp.zeros_like(before)
    scale_all[...] = jnp.zeros_like(scale_all)
    kappa_buf[...] = jnp.zeros_like(kappa_buf)
    mu_buf[...] = jnp.zeros_like(mu_buf)
    force_buf[...] = jnp.zeros_like(force_buf)
    for i in (4, 5, 6, 10):
        loads[i].wait()
    rows[0:elems, 0:125] = conn[...]
    rows[elems : elems + 1, :] = receivers[...]
    for which, ref in enumerate((lower, upper)):
        for k in range(face_chunks):
            size = min(LANES, face - k * LANES)
            at = elems + 1 + which * face_chunks + k
            rows[at : at + 1, 0:size] = ref[:, k * LANES : k * LANES + size]
    columns = (rows[...].astype(f32).T.astype(jnp.int32) & (WIDE - 1)).astype(f32).astype(bf16)

    lane = lax.broadcasted_iota(jnp.int32, (LANES, WIDE), 1).astype(f32).astype(bf16)
    one = jnp.ones((LANES, WIDE), bf16)
    none = jnp.zeros((LANES, WIDE), bf16)
    half = lax.broadcasted_iota(jnp.int32, (16, LANES), 0) >> 3
    empty = jnp.zeros((16, LANES), bf16)

    def spread(at):
        low = jnp.broadcast_to(columns[:, at : at + 1], (LANES, WIDE))
        onehot[at * LANES : (at + 1) * LANES, :] = jnp.where(lane == low, one, none)

    def take(table, low):
        return jnp.take_along_axis(table, low, axis=1, mode="promise_in_bounds")

    def lookup(tables, index, count):
        low = index & (LANES - 1)
        high = index >> 7
        outs = [jnp.zeros(index.shape, f32) for _ in tables]
        for k in range(count):
            here = high == k
            for t, table in enumerate(tables):
                outs[t] = jnp.where(here, take(table(k), low), outs[t])
        return outs

    def row_of(ref, c):
        return lambda k: jnp.broadcast_to(ref[c : c + 1, lanes_of(k)], tile)

    def place(at, value):
        high = jnp.broadcast_to(rows[at : at + 1, :] >> 8, (16, LANES)) - half
        high = high.astype(f32).astype(bf16)
        parts = two_parts(jnp.concatenate([value, value], 0))
        for k in range(part_rows // 16):
            here = high == jnp.full((16, LANES), 2 * k, bf16)
            for s, part in enumerate(parts):
                row = s * part_rows + 16 * k
                left[row : row + 16, lanes_of(at)] = jnp.where(here, part, empty)

    def deposit(start, stop, out):
        span = slice(start * LANES, stop * LANES)
        total = jnp.dot(left[:, span], onehot[span, :], preferred_element_type=f32)
        total = total[0:part_rows] + total[part_rows:]
        for k in range(slabs):
            out[:, k * WIDE : (k + 1) * WIDE] = total[8 * k : 8 * k + 8]

    def element_index(group):
        return rows[group * 8 : group * 8 + 8, :]

    def at_elements(ref):
        parts = [[] for _ in range(6)]
        for group in range(elems // 8):
            got = lookup([row_of(ref, c) for c in range(6)], element_index(group), chunks)
            for c in range(6):
                parts[c].append(got[c])
        return parts

    for i in (0, 2, 12, 7, 8, 13, 11, 1, 3, 9):
        loads[i].wait()
    for c in range(3):
        waves[c : c + 1, 0:points] = fwd_now[c]
        waves[3 + c : 4 + c, 0:points] = adj_now[c]
    parts = at_elements(waves)
    for e in range(elems + 1):
        spread(e)
    kappa_buf[:, 0:125] = bulk_mod[...]
    mu_buf[:, 0:125] = shear_mod[...]
    kappa = kappa_buf[...]
    mu = mu_buf[...]

    span = ahead.shape[0] // 3
    forward_table = jnp.concatenate([ahead[i * span : (i + 1) * span, :] for i in range(3)], 1)
    bulk = jnp.zeros((elems, LANES), f32)
    shear = jnp.zeros((elems, LANES), f32)
    pending = []
    for step in range(STEPS):
        values = jnp.concatenate([piece for part in parts for piece in part], 0)
        grads = product(values, forward_table)

        def grad(i, c):
            return grads[c * elems : (c + 1) * elems, i * LANES : (i + 1) * LANES]

        divs, devs = [], []
        for f in range(2):
            g = [[grad(i, f * 3 + j) for j in range(3)] for i in range(3)]
            div = g[0][0] + g[1][1] + g[2][2]
            third = div * (1.0 / 3.0)
            dev = {(i, i): g[i][i] - third for i in range(3)}
            for i, j in ((0, 1), (0, 2), (1, 2)):
                dev[i, j] = 0.5 * (g[i][j] + g[j][i])
            divs.append(div)
            devs.append(dev)
            pressure = kappa * div
            for (i, j), term in dev.items():
                tension = 2.0 * mu * term
                if i == j:
                    tension = tension + pressure
                for first, second in ((i, j), (j, i))[: 1 + (i != j)]:
                    c = f * 3 + second
                    stress_buf[c * elems : (c + 1) * elems, lanes_of(first)] = tension

        force_buf[0 : 6 * elems, :] = product(stress_buf[...], back[...])
        for e in range(elems):
            place(e, force_buf[pl.ds(e, 8, stride=elems), :])
        injected = jnp.concatenate(
            [jnp.zeros((3, LANES), f32), source[0, :, step, :], jnp.zeros((2, LANES), f32)], 0
        )
        place(elems, injected)
        deposit(0, elems + 1, forces)

        copies = []
        if step == 0:
            pl.semaphore_wait(barrier, 2 + n_event - 1)
        for which, other in ((0, previous), (1, following)):
            for k in range(face_chunks):
                at = elems + 1 + which * face_chunks + k
                index = jnp.broadcast_to(rows[at : at + 1, :], tile)
                face_send[step, which, :, lanes_of(k)] = lookup(
                    [lambda q: forces[:, lanes_of(q)]], index, chunks
                )[0]
            copy = pltpu.make_async_remote_copy(
                src_ref=face_send.at[step, which],
                dst_ref=face_recv.at[step, 1 - which],
                send_sem=face_ssem.at[step, which],
                recv_sem=face_rsem.at[step, 1 - which],
                device_id={"mesh": other, "event": my_event},
                device_id_type=MESH,
            )
            copy.start()
            copies.append(copy)

        bulk = bulk - KERNEL_WEIGHT * kappa * divs[0] * divs[1]
        both = {key: devs[0][key] * devs[1][key] for key in devs[0]}
        paired = both[0, 0] + both[1, 1] + both[2, 2]
        paired = paired + 2.0 * (both[0, 1] + both[0, 2] + both[1, 2])
        shear = shear - 2.0 * KERNEL_WEIGHT * mu * paired

        if step == STEPS - 1:
            for owner in range(n_event):
                kern_send[owner, 0] = bulk[owner * cols : (owner + 1) * cols]
                kern_send[owner, 1] = shear[owner * cols : (owner + 1) * cols]
            for hop in range(1, n_event):
                peer = lax.rem(my_event + hop, n_event)
                copy = pltpu.make_async_remote_copy(
                    src_ref=kern_send.at[peer],
                    dst_ref=kern_recv.at[hop - 1],
                    send_sem=kern_ssem.at[hop - 1],
                    recv_sem=kern_rsem.at[hop - 1],
                    device_id={"mesh": me, "event": peer},
                    device_id_type=MESH,
                )
                copy.start()
                pending.append(copy)

        if step == 0:
            for c in range(3):
                before[c : c + 1, 0:points] = fwd_prev[c]
                before[3 + c : 4 + c, 0:points] = adj_prev[c]
            scale_all[:, 0:points] = jnp.broadcast_to(scale[...].reshape(1, points), (8, points))
            later[...] = 2.0 * waves[...] - before[...] + scale_all[...] * forces[...]
            parts = at_elements(later)
            number = lax.broadcasted_iota(jnp.int32, tile, 1)
            for which, inside in ((0, me > 0), (1, me < n_mesh - 1)):
                for k in range(face_chunks):
                    at = elems + 1 + which * face_chunks + k
                    spread(at)
                    slot = number + ((which * face_chunks + k) * LANES + 1)
                    place(at, jnp.where(inside, slot.astype(f32), 0.0))
            deposit(elems + 1, elems + 1 + 2 * face_chunks, slots)
            found = [
                lookup([row_of(slots, 0)], element_index(group), chunks)[0]
                for group in range(elems // 8)
            ]
            factors = lookup([row_of(scale_all, 0)], rows[elems : elems + 8, :], chunks)[0]
            for copy in copies:
                copy.wait()
            for which in range(2):
                for k in range(face_chunks):
                    at = 1 + which * face_chunks + k
                    span = lanes_of(k)
                    face_scaled[which, :, span] = (
                        face_recv[step, which, :, span] * factors[at : at + 1, :]
                    )
            for group in range(elems // 8):
                which = 0 if group < elems // 16 else 1
                index = found[group].astype(jnp.int32) - (1 + which * face_chunks * LANES)
                got = lookup(
                    [row_of(face_scaled.at[which], c) for c in range(6)], index, face_chunks
                )
                for c in range(6):
                    parts[c][group] = parts[c][group] + got[c]
        else:

            def arrived(at, q):
                index = slots[:, lanes_of(q)].astype(jnp.int32) - 1
                return lookup(
                    [
                        lambda k: face_recv[
                            at, k // face_chunks, :, lanes_of(k % face_chunks)
                        ]
                    ],
                    index,
                    2 * face_chunks,
                )[0]

            for q in range(chunks):
                span = lanes_of(q)
                now = later[:, span] + scale_all[:, span] * arrived(0, q)
                before[:, span] = (
                    2.0 * now - waves[:, span] + scale_all[:, span] * forces[:, span]
                )
            for copy in copies:
                copy.wait()
            for q in range(chunks):
                span = lanes_of(q)
                later[:, span] = before[:, span] + scale_all[:, span] * arrived(1, q)

    for c in range(3):
        fwd_out[c] = later[c : c + 1, 0:points]
        adj_out[c] = later[3 + c : 4 + c, 0:points]
    owned = kern_send[my_event]
    for copy in pending:
        copy.wait()
    for hop in range(1, n_event):
        owned = owned + kern_recv[hop - 1]
    kern_out[...] = owned[:, :, 0:125]


def copy_out(*refs):
    count = len(refs) // 2
    sem = refs[-1]
    copies = [pltpu.make_async_copy(refs[i], refs[count + i], sem.at[i]) for i in range(count)]
    for copy in copies:
        copy.start()
    for copy in copies:
        copy.wait()


def hand_out(results):
    count = len(results)
    return pl.pallas_call(
        copy_out,
        out_shape=tuple(jax.ShapeDtypeStruct(v.shape, v.dtype) for v in results),
        in_specs=[pl.BlockSpec(memory_space=pltpu.VMEM)] * count,
        out_specs=[pl.BlockSpec(memory_space=pltpu.HBM)] * count,
        scratch_shapes=[pltpu.SemaphoreType.DMA((count,))],
        compiler_params=pltpu.CompilerParams(vmem_limit_bytes=1024 * 1024),
    )(*results)


def shards(
    n_mesh,
    n_event,
    forward_now,
    forward_prev,
    adjoint_now,
    adjoint_prev,
    connectivity,
    lower_face,
    upper_face,
    bulk_modulus,
    shear_modulus,
    step_scale,
    receiver_points,
    adjoint_source,
):
    points = forward_now.shape[2]
    face = lower_face.shape[1]
    elems = connectivity.shape[1]
    cols = elems // n_event
    slabs = -(-points // WIDE)
    slabs += slabs % 2
    width = slabs * WIDE
    face_chunks = -(-face // LANES)
    blocks = elems + 1 + 2 * face_chunks
    f32 = jnp.float32
    ahead, back = cube_tables()
    fields = [v.transpose(1, 0, 2) for v in (forward_now, forward_prev, adjoint_now, adjoint_prev)]
    operands = (
        *fields,
        connectivity.T,
        lower_face,
        upper_face,
        bulk_modulus.T,
        shear_modulus.T,
        step_scale,
        receiver_points.reshape(1, -1),
        adjoint_source.transpose(0, 2, 1, 3),
        jnp.asarray(np.concatenate(np.split(ahead, 3, 1), 0)),
        jnp.asarray(back),
    )
    state = pltpu.VMEM((8, width), f32)
    moduli = pltpu.VMEM((elems, LANES), f32)
    peers = max(n_event - 1, 1)
    call = pl.pallas_call(
        functools.partial(body, n_mesh, n_event, points, face, elems),
        out_shape=(
            pltpu.VMEM(fields[0].shape, f32),
            pltpu.VMEM(fields[2].shape, f32),
            pltpu.VMEM((2, cols, 125), f32),
        ),
        in_specs=[pl.BlockSpec(memory_space=pltpu.HBM)] * 14,
        out_specs=[pl.BlockSpec(memory_space=pltpu.VMEM)] * 3,
        scratch_shapes=[
            *[pltpu.VMEM(v.shape, v.dtype) for v in operands],
            pltpu.SemaphoreType.DMA((14,)),
            state,
            state,
            state,
            state,
            state,
            state,
            moduli,
            moduli,
            pltpu.VMEM((LANES, LANES), jnp.int32),
            pltpu.VMEM((blocks * LANES, WIDE), jnp.bfloat16),
            pltpu.VMEM((2 * slabs * 8, blocks * LANES), jnp.bfloat16),
            pltpu.VMEM((6 * elems, 3 * LANES), f32),
            pltpu.VMEM((8 * elems, LANES), f32),
            pltpu.VMEM((STEPS, 2, 8, face_chunks * LANES), f32),
            pltpu.VMEM((STEPS, 2, 8, face_chunks * LANES), f32),
            pltpu.VMEM((2, 8, face_chunks * LANES), f32),
            pltpu.VMEM((n_event, 2, cols, LANES), f32),
            pltpu.VMEM((peers, 2, cols, LANES), f32),
            pltpu.SemaphoreType.DMA((STEPS, 2)),
            pltpu.SemaphoreType.DMA((STEPS, 2)),
            pltpu.SemaphoreType.DMA((peers,)),
            pltpu.SemaphoreType.DMA((peers,)),
        ],
        compiler_params=pltpu.CompilerParams(
            collective_id=0, has_side_effects=True, vmem_limit_bytes=60 * 1024 * 1024
        ),
    )
    forward, adjoint, kernels = hand_out(call(*operands))
    return (forward.transpose(1, 0, 2), adjoint.transpose(1, 0, 2), kernels.transpose(0, 2, 1))


def solution(mesh):
    placed = (
        P("event", None, "mesh"),
        P("event", None, "mesh"),
        P("event", None, "mesh"),
        P("event", None, "mesh"),
        P(None, "mesh"),
        P("mesh", None),
        P("mesh", None),
        P(None, "mesh"),
        P(None, "mesh"),
        P("mesh"),
        P("mesh"),
        P("event", None, None, "mesh"),
    )
    return jax.shard_map(
        functools.partial(shards, mesh.shape["mesh"], mesh.shape["event"]),
        mesh=mesh,
        in_specs=placed,
        out_specs=(
            P("event", None, "mesh"),
            P("event", None, "mesh"),
            P(None, None, ("mesh", "event")),
        ),
        check_vma=False,
    )
```

```python
import functools
import math

import jax
import jax.numpy as jnp
import numpy as np
from jax import lax
from jax.experimental import pallas as pl
from jax.experimental.pallas import tpu as pltpu
from jax.sharding import PartitionSpec as P

STEPS = 2
LANES = 128
WIDE = 256
KERNEL_WEIGHT = 0.02
MESH = pl.DeviceIdType.MESH


def derivative_table():
    root = math.sqrt(3.0 / 7.0)
    points = [-1.0, -root, 0.0, root, 1.0]
    legendre = [(35.0 * x**4 - 30.0 * x**2 + 3.0) / 8.0 for x in points]
    table = np.zeros((5, 5))
    for row in range(5):
        for column in range(5):
            if row != column:
                table[row, column] = (
                    legendre[row] / legendre[column] / (points[row] - points[column])
                )
    table[0, 0] = -2.5
    table[4, 4] = 2.5
    return table


def cube_tables():
    deriv = derivative_table()
    line = np.array([0.1, 49.0 / 90.0, 32.0 / 45.0, 49.0 / 90.0, 0.1])
    cube = (line[:, None, None] * line[None, :, None] * line[None, None, :]).reshape(125)
    along = [
        np.kron(np.eye(25), deriv),
        np.kron(np.eye(5), np.kron(deriv, np.eye(5))),
        np.kron(deriv, np.eye(25)),
    ]
    ahead = np.zeros((LANES, 3 * LANES))
    back = np.zeros((3 * LANES, LANES))
    for i in range(3):
        ahead[:125, i * LANES : i * LANES + 125] = along[i].T
        back[i * LANES : i * LANES + 125, :125] = -along[i] * cube[:, None]
    return stacked(ahead), stacked(back)


def stacked(table):
    rest = table.astype(np.float32)
    parts = []
    for _ in range(2):
        part = rest.astype(jnp.bfloat16)
        rest = rest - part.astype(np.float32)
        parts.append(part)
    first, second = parts
    return np.concatenate([first, first, second], 0)


def two_parts(value):
    first = value.astype(jnp.bfloat16)
    second = (value - first.astype(jnp.float32)).astype(jnp.bfloat16)
    return first, second


def product(value, table):
    first, second = two_parts(value)
    wide = jnp.concatenate([first, second, first], 1)
    return jnp.dot(wide, table, preferred_element_type=jnp.float32)


def body(n_mesh, n_event, points, face, elems, *refs):
    sources, refs = refs[:14], refs[14:]
    (fwd_out, adj_out, kern_out), refs = refs[:3], refs[3:]
    held, refs = refs[:14], refs[14:]
    (
        fwd_now,
        fwd_prev,
        adj_now,
        adj_prev,
        conn,
        lower,
        upper,
        bulk_mod,
        shear_mod,
        scale,
        receivers,
        source,
        ahead,
        back,
    ) = held
    (
        load_sem,
        waves,
        before,
        later,
        scale_all,
        forces,
        slots,
        kappa_buf,
        mu_buf,
        rows,
        onehot,
        left,
        stress_buf,
        force_buf,
        face_send,
        face_recv,
        face_scaled,
        kern_send,
        kern_recv,
        face_ssem,
        face_rsem,
        kern_ssem,
        kern_rsem,
    ) = refs
    loads = [
        pltpu.make_async_copy(src, dst, load_sem.at[i])
        for i, (src, dst) in enumerate(zip(sources, held))
    ]
    for i in (4, 5, 6, 10, 0, 2, 12, 7, 8, 13, 11, 1, 3, 9):
        loads[i].start()

    me = lax.axis_index("mesh")
    my_event = lax.axis_index("event")
    following = lax.rem(me + 1, n_mesh)
    previous = lax.rem(me + n_mesh - 1, n_mesh)
    has_previous = me > 0
    has_following = me < n_mesh - 1
    face_recv[...] = jnp.zeros_like(face_recv)
    barrier = pltpu.get_barrier_semaphore()
    for other in (following, previous):
        pl.semaphore_signal(
            barrier, inc=1, device_id={"mesh": other, "event": my_event}, device_id_type=MESH
        )
    for hop in range(1, n_event):
        peer = lax.rem(my_event + hop, n_event)
        pl.semaphore_signal(
            barrier, inc=1, device_id={"mesh": me, "event": peer}, device_id_type=MESH
        )

    f32 = jnp.float32
    bf16 = jnp.bfloat16
    chunks = -(-points // LANES)
    slabs = waves.shape[1] // WIDE
    face_chunks = face_send.shape[3] // LANES
    part_rows = left.shape[0] // 2
    cols = elems // n_event
    tile = (8, LANES)

    def lanes_of(k):
        return slice(k * LANES, (k + 1) * LANES)

    rows[...] = jnp.full(rows.shape, -1, jnp.int32)
    waves[...] = jnp.zeros_like(waves)
    before[...] = jnp.zeros_like(before)
    scale_all[...] = jnp.zeros_like(scale_all)
    kappa_buf[...] = jnp.zeros_like(kappa_buf)
    mu_buf[...] = jnp.zeros_like(mu_buf)
    force_buf[...] = jnp.zeros_like(force_buf)
    for i in (4, 5, 6, 10):
        loads[i].wait()
    rows[0:elems, 0:125] = conn[...]
    rows[elems : elems + 1, :] = receivers[...]
    for which, ref in enumerate((lower, upper)):
        for k in range(face_chunks):
            size = min(LANES, face - k * LANES)
            at = elems + 1 + which * face_chunks + k
            rows[at : at + 1, 0:size] = ref[:, k * LANES : k * LANES + size]
    columns = (rows[...].astype(f32).T.astype(jnp.int32) & (WIDE - 1)).astype(f32).astype(bf16)

    lane = lax.broadcasted_iota(jnp.int32, (LANES, WIDE), 1).astype(f32).astype(bf16)
    one = jnp.ones((LANES, WIDE), bf16)
    none = jnp.zeros((LANES, WIDE), bf16)
    half = lax.broadcasted_iota(jnp.int32, (16, LANES), 0) >> 3
    empty = jnp.zeros((16, LANES), bf16)

    def spread(at):
        low = jnp.broadcast_to(columns[:, at : at + 1], (LANES, WIDE))
        onehot[at * LANES : (at + 1) * LANES, :] = jnp.where(lane == low, one, none)

    def take(table, low):
        return jnp.take_along_axis(table, low, axis=1, mode="promise_in_bounds")

    def lookup(tables, index, count):
        low = index & (LANES - 1)
        high = index >> 7
        outs = [jnp.zeros(index.shape, f32) for _ in tables]
        for k in range(count):
            here = high == k
            for t, table in enumerate(tables):
                outs[t] = jnp.where(here, take(table(k), low), outs[t])
        return outs

    def row_of(ref, c):
        return lambda k: jnp.broadcast_to(ref[c : c + 1, lanes_of(k)], tile)

    def place(at, value):
        high = jnp.broadcast_to(rows[at : at + 1, :] >> 8, (16, LANES)) - half
        high = high.astype(f32).astype(bf16)
        parts = two_parts(jnp.concatenate([value, value], 0))
        for k in range(part_rows // 16):
            here = high == jnp.full((16, LANES), 2 * k, bf16)
            for s, part in enumerate(parts):
                row = s * part_rows + 16 * k
                left[row : row + 16, lanes_of(at)] = jnp.where(here, part, empty)

    def deposit(start, stop, out):
        span = slice(start * LANES, stop * LANES)
        total = jnp.dot(left[:, span], onehot[span, :], preferred_element_type=f32)
        total = total[0:part_rows] + total[part_rows:]
        for k in range(slabs):
            out[:, k * WIDE : (k + 1) * WIDE] = total[8 * k : 8 * k + 8]

    def finish(copies):
        @pl.when(has_previous)
        def _():
            copies[0].wait_send()
            copies[1].wait_recv()

        @pl.when(has_following)
        def _():
            copies[1].wait_send()
            copies[0].wait_recv()

    def element_index(group):
        return rows[group * 8 : group * 8 + 8, :]

    def at_elements(ref):
        parts = [[] for _ in range(6)]
        for group in range(elems // 8):
            got = lookup([row_of(ref, c) for c in range(6)], element_index(group), chunks)
            for c in range(6):
                parts[c].append(got[c])
        return parts

    for i in (0, 2):
        loads[i].wait()
    for c in range(3):
        waves[c : c + 1, 0:points] = fwd_now[c]
        waves[3 + c : 4 + c, 0:points] = adj_now[c]
    parts = at_elements(waves)
    for e in range(elems + 1):
        spread(e)
    for i in (12, 7, 8):
        loads[i].wait()
    kappa_buf[:, 0:125] = bulk_mod[...]
    mu_buf[:, 0:125] = shear_mod[...]
    kappa = kappa_buf[...]
    mu = mu_buf[...]

    span = ahead.shape[0] // 3
    forward_table = jnp.concatenate([ahead[i * span : (i + 1) * span, :] for i in range(3)], 1)
    bulk = jnp.zeros((elems, LANES), f32)
    shear = jnp.zeros((elems, LANES), f32)
    pending = []
    for step in range(STEPS):
        values = jnp.concatenate([piece for part in parts for piece in part], 0)
        grads = product(values, forward_table)

        def grad(i, c):
            return grads[c * elems : (c + 1) * elems, i * LANES : (i + 1) * LANES]

        divs, devs = [], []
        for f in range(2):
            g = [[grad(i, f * 3 + j) for j in range(3)] for i in range(3)]
            div = g[0][0] + g[1][1] + g[2][2]
            third = div * (1.0 / 3.0)
            dev = {(i, i): g[i][i] - third for i in range(3)}
            for i, j in ((0, 1), (0, 2), (1, 2)):
                dev[i, j] = 0.5 * (g[i][j] + g[j][i])
            divs.append(div)
            devs.append(dev)
            pressure = kappa * div
            for (i, j), term in dev.items():
                tension = 2.0 * mu * term
                if i == j:
                    tension = tension + pressure
                for first, second in ((i, j), (j, i))[: 1 + (i != j)]:
                    c = f * 3 + second
                    stress_buf[c * elems : (c + 1) * elems, lanes_of(first)] = tension

        if step == 0:
            loads[13].wait()
        force_buf[0 : 6 * elems, :] = product(stress_buf[...], back[...])
        for e in range(elems):
            place(e, force_buf[pl.ds(e, 8, stride=elems), :])
        if step == 0:
            loads[11].wait()
        injected = jnp.concatenate(
            [jnp.zeros((3, LANES), f32), source[0, :, step, :], jnp.zeros((2, LANES), f32)], 0
        )
        place(elems, injected)
        deposit(0, elems + 1, forces)

        copies = []
        if step == 0:
            pl.semaphore_wait(barrier, 2 + n_event - 1)
        for which, other in ((0, previous), (1, following)):
            for k in range(face_chunks):
                at = elems + 1 + which * face_chunks + k
                index = jnp.broadcast_to(rows[at : at + 1, :], tile)
                face_send[step, which, :, lanes_of(k)] = lookup(
                    [lambda q: forces[:, lanes_of(q)]], index, chunks
                )[0]
            copy = pltpu.make_async_remote_copy(
                src_ref=face_send.at[step, which],
                dst_ref=face_recv.at[step, 1 - which],
                send_sem=face_ssem.at[step, which],
                recv_sem=face_rsem.at[step, 1 - which],
                device_id={"mesh": other, "event": my_event},
                device_id_type=MESH,
            )
            copies.append(copy)
        pl.when(has_previous)(copies[0].start)
        pl.when(has_following)(copies[1].start)

        bulk = bulk - KERNEL_WEIGHT * kappa * divs[0] * divs[1]
        both = {key: devs[0][key] * devs[1][key] for key in devs[0]}
        paired = both[0, 0] + both[1, 1] + both[2, 2]
        paired = paired + 2.0 * (both[0, 1] + both[0, 2] + both[1, 2])
        shear = shear - 2.0 * KERNEL_WEIGHT * mu * paired

        if step == STEPS - 1:
            for owner in range(n_event):
                kern_send[owner, 0] = bulk[owner * cols : (owner + 1) * cols]
                kern_send[owner, 1] = shear[owner * cols : (owner + 1) * cols]
            for hop in range(1, n_event):
                peer = lax.rem(my_event + hop, n_event)
                copy = pltpu.make_async_remote_copy(
                    src_ref=kern_send.at[peer],
                    dst_ref=kern_recv.at[hop - 1],
                    send_sem=kern_ssem.at[hop - 1],
                    recv_sem=kern_rsem.at[hop - 1],
                    device_id={"mesh": me, "event": peer},
                    device_id_type=MESH,
                )
                copy.start()
                pending.append(copy)

        if step == 0:
            for i in (1, 3, 9):
                loads[i].wait()
            for c in range(3):
                before[c : c + 1, 0:points] = fwd_prev[c]
                before[3 + c : 4 + c, 0:points] = adj_prev[c]
            scale_all[:, 0:points] = jnp.broadcast_to(scale[...].reshape(1, points), (8, points))
            later[...] = 2.0 * waves[...] - before[...] + scale_all[...] * forces[...]
            parts = at_elements(later)
            number = lax.broadcasted_iota(jnp.int32, tile, 1)
            for which, inside in ((0, has_previous), (1, has_following)):
                for k in range(face_chunks):
                    at = elems + 1 + which * face_chunks + k
                    spread(at)
                    slot = number + ((which * face_chunks + k) * LANES + 1)
                    place(at, jnp.where(inside, slot.astype(f32), 0.0))
            deposit(elems + 1, elems + 1 + 2 * face_chunks, slots)
            found = [
                lookup([row_of(slots, 0)], element_index(group), chunks)[0]
                for group in range(elems // 8)
            ]
            factors = lookup([row_of(scale_all, 0)], rows[elems : elems + 8, :], chunks)[0]
            finish(copies)
            for which in range(2):
                for k in range(face_chunks):
                    at = 1 + which * face_chunks + k
                    span = lanes_of(k)
                    face_scaled[which, :, span] = (
                        face_recv[step, which, :, span] * factors[at : at + 1, :]
                    )
            for group in range(elems // 8):
                which = 0 if group < elems // 16 else 1
                index = found[group].astype(jnp.int32) - (1 + which * face_chunks * LANES)
                got = lookup(
                    [row_of(face_scaled.at[which], c) for c in range(6)], index, face_chunks
                )
                for c in range(6):
                    parts[c][group] = parts[c][group] + got[c]
        else:

            def arrived(at, q):
                index = slots[:, lanes_of(q)].astype(jnp.int32) - 1
                return lookup(
                    [
                        lambda k: face_recv[
                            at, k // face_chunks, :, lanes_of(k % face_chunks)
                        ]
                    ],
                    index,
                    2 * face_chunks,
                )[0]

            for q in range(chunks):
                span = lanes_of(q)
                now = later[:, span] + scale_all[:, span] * arrived(0, q)
                before[:, span] = (
                    2.0 * now - waves[:, span] + scale_all[:, span] * forces[:, span]
                )
            finish(copies)
            for q in range(chunks):
                span = lanes_of(q)
                later[:, span] = before[:, span] + scale_all[:, span] * arrived(1, q)

    for c in range(3):
        fwd_out[c] = later[c : c + 1, 0:points]
        adj_out[c] = later[3 + c : 4 + c, 0:points]
    owned = kern_send[my_event]
    for copy in pending:
        copy.wait()
    for hop in range(1, n_event):
        owned = owned + kern_recv[hop - 1]
    kern_out[...] = owned[:, :, 0:125]


def copy_out(*refs):
    count = len(refs) // 2
    sem = refs[-1]
    copies = [pltpu.make_async_copy(refs[i], refs[count + i], sem.at[i]) for i in range(count)]
    for copy in copies:
        copy.start()
    for copy in copies:
        copy.wait()


def hand_out(results):
    count = len(results)
    return pl.pallas_call(
        copy_out,
        out_shape=tuple(jax.ShapeDtypeStruct(v.shape, v.dtype) for v in results),
        in_specs=[pl.BlockSpec(memory_space=pltpu.VMEM)] * count,
        out_specs=[pl.BlockSpec(memory_space=pltpu.HBM)] * count,
        scratch_shapes=[pltpu.SemaphoreType.DMA((count,))],
        compiler_params=pltpu.CompilerParams(vmem_limit_bytes=1024 * 1024),
    )(*results)


def shards(
    n_mesh,
    n_event,
    forward_now,
    forward_prev,
    adjoint_now,
    adjoint_prev,
    connectivity,
    lower_face,
    upper_face,
    bulk_modulus,
    shear_modulus,
    step_scale,
    receiver_points,
    adjoint_source,
):
    points = forward_now.shape[2]
    face = lower_face.shape[1]
    elems = connectivity.shape[1]
    cols = elems // n_event
    slabs = -(-points // WIDE)
    slabs += slabs % 2
    width = slabs * WIDE
    face_chunks = -(-face // LANES)
    blocks = elems + 1 + 2 * face_chunks
    f32 = jnp.float32
    ahead, back = cube_tables()
    fields = [v.transpose(1, 0, 2) for v in (forward_now, forward_prev, adjoint_now, adjoint_prev)]
    operands = (
        *fields,
        connectivity.T,
        lower_face,
        upper_face,
        bulk_modulus.T,
        shear_modulus.T,
        step_scale,
        receiver_points.reshape(1, -1),
        adjoint_source.transpose(0, 2, 1, 3),
        jnp.asarray(np.concatenate(np.split(ahead, 3, 1), 0)),
        jnp.asarray(back),
    )
    state = pltpu.VMEM((8, width), f32)
    moduli = pltpu.VMEM((elems, LANES), f32)
    peers = max(n_event - 1, 1)
    call = pl.pallas_call(
        functools.partial(body, n_mesh, n_event, points, face, elems),
        out_shape=(
            pltpu.VMEM(fields[0].shape, f32),
            pltpu.VMEM(fields[2].shape, f32),
            pltpu.VMEM((2, cols, 125), f32),
        ),
        in_specs=[pl.BlockSpec(memory_space=pltpu.HBM)] * 14,
        out_specs=[pl.BlockSpec(memory_space=pltpu.VMEM)] * 3,
        scratch_shapes=[
            *[pltpu.VMEM(v.shape, v.dtype) for v in operands],
            pltpu.SemaphoreType.DMA((14,)),
            state,
            state,
            state,
            state,
            state,
            state,
            moduli,
            moduli,
            pltpu.VMEM((LANES, LANES), jnp.int32),
            pltpu.VMEM((blocks * LANES, WIDE), jnp.bfloat16),
            pltpu.VMEM((2 * slabs * 8, blocks * LANES), jnp.bfloat16),
            pltpu.VMEM((6 * elems, 3 * LANES), f32),
            pltpu.VMEM((8 * elems, LANES), f32),
            pltpu.VMEM((STEPS, 2, 8, face_chunks * LANES), f32),
            pltpu.VMEM((STEPS, 2, 8, face_chunks * LANES), f32),
            pltpu.VMEM((2, 8, face_chunks * LANES), f32),
            pltpu.VMEM((n_event, 2, cols, LANES), f32),
            pltpu.VMEM((peers, 2, cols, LANES), f32),
            pltpu.SemaphoreType.DMA((STEPS, 2)),
            pltpu.SemaphoreType.DMA((STEPS, 2)),
            pltpu.SemaphoreType.DMA((peers,)),
            pltpu.SemaphoreType.DMA((peers,)),
        ],
        compiler_params=pltpu.CompilerParams(
            collective_id=0, has_side_effects=True, vmem_limit_bytes=60 * 1024 * 1024
        ),
    )
    forward, adjoint, kernels = hand_out(call(*operands))
    return (forward.transpose(1, 0, 2), adjoint.transpose(1, 0, 2), kernels.transpose(0, 2, 1))


def solution(mesh):
    placed = (
        P("event", None, "mesh"),
        P("event", None, "mesh"),
        P("event", None, "mesh"),
        P("event", None, "mesh"),
        P(None, "mesh"),
        P("mesh", None),
        P("mesh", None),
        P(None, "mesh"),
        P(None, "mesh"),
        P("mesh"),
        P("mesh"),
        P("event", None, None, "mesh"),
    )
    return jax.shard_map(
        functools.partial(shards, mesh.shape["mesh"], mesh.shape["event"]),
        mesh=mesh,
        in_specs=placed,
        out_specs=(
            P("event", None, "mesh"),
            P("event", None, "mesh"),
            P(None, None, ("mesh", "event")),
        ),
        check_vma=False,
    )
```

```python
import functools
import math

import jax
import jax.numpy as jnp
import numpy as np
from jax import lax
from jax.experimental import pallas as pl
from jax.experimental.pallas import tpu as pltpu
from jax.sharding import PartitionSpec as P

STEPS = 2
LANES = 128
WIDE = 256
KERNEL_WEIGHT = 0.02
MESH = pl.DeviceIdType.MESH


def derivative_table():
    root = math.sqrt(3.0 / 7.0)
    points = [-1.0, -root, 0.0, root, 1.0]
    legendre = [(35.0 * x**4 - 30.0 * x**2 + 3.0) / 8.0 for x in points]
    table = np.zeros((5, 5))
    for row in range(5):
        for column in range(5):
            if row != column:
                table[row, column] = (
                    legendre[row] / legendre[column] / (points[row] - points[column])
                )
    table[0, 0] = -2.5
    table[4, 4] = 2.5
    return table


def cube_tables():
    deriv = derivative_table()
    line = np.array([0.1, 49.0 / 90.0, 32.0 / 45.0, 49.0 / 90.0, 0.1])
    cube = (line[:, None, None] * line[None, :, None] * line[None, None, :]).reshape(125)
    along = [
        np.kron(np.eye(25), deriv),
        np.kron(np.eye(5), np.kron(deriv, np.eye(5))),
        np.kron(deriv, np.eye(25)),
    ]
    ahead = np.zeros((LANES, 3 * LANES))
    back = np.zeros((3 * LANES, LANES))
    for i in range(3):
        ahead[:125, i * LANES : i * LANES + 125] = along[i].T
        back[i * LANES : i * LANES + 125, :125] = -along[i] * cube[:, None]
    return stacked(ahead), stacked(back)


def stacked(table):
    rest = table.astype(np.float32)
    parts = []
    for _ in range(2):
        part = rest.astype(jnp.bfloat16)
        rest = rest - part.astype(np.float32)
        parts.append(part)
    first, second = parts
    return np.concatenate([first, first, second], 0)


def two_parts(value):
    first = value.astype(jnp.bfloat16)
    second = (value - first.astype(jnp.float32)).astype(jnp.bfloat16)
    return first, second


def product(value, table):
    first, second = two_parts(value)
    wide = jnp.concatenate([first, second, first], 1)
    return jnp.dot(wide, table, preferred_element_type=jnp.float32)


def body(n_mesh, n_event, points, face, elems, *refs):
    sources, refs = refs[:14], refs[14:]
    (fwd_out, adj_out, kern_out), refs = refs[:3], refs[3:]
    held, refs = refs[:14], refs[14:]
    (
        fwd_now,
        fwd_prev,
        adj_now,
        adj_prev,
        conn,
        lower,
        upper,
        bulk_mod,
        shear_mod,
        scale,
        receivers,
        source,
        ahead,
        back,
    ) = held
    (
        load_sem,
        waves,
        before,
        later,
        scale_all,
        forces,
        slots,
        kappa_buf,
        mu_buf,
        rows,
        onehot,
        left,
        stress_buf,
        force_buf,
        face_send,
        face_recv,
        face_scaled,
        kern_send,
        kern_recv,
        face_ssem,
        face_rsem,
        kern_ssem,
        kern_rsem,
    ) = refs
    loads = [
        pltpu.make_async_copy(src, dst, load_sem.at[i])
        for i, (src, dst) in enumerate(zip(sources, held))
    ]
    for i in (4, 5, 6, 10, 0, 2, 12, 7, 8, 13, 11, 1, 3, 9):
        loads[i].start()

    me = lax.axis_index("mesh")
    my_event = lax.axis_index("event")
    following = lax.rem(me + 1, n_mesh)
    previous = lax.rem(me + n_mesh - 1, n_mesh)
    has_previous = me > 0
    has_following = me < n_mesh - 1
    face_recv[...] = jnp.zeros_like(face_recv)
    barrier = pltpu.get_barrier_semaphore()
    for other in (following, previous):
        pl.semaphore_signal(
            barrier, inc=1, device_id={"mesh": other, "event": my_event}, device_id_type=MESH
        )
    for hop in range(1, n_event):
        peer = lax.rem(my_event + hop, n_event)
        pl.semaphore_signal(
            barrier, inc=1, device_id={"mesh": me, "event": peer}, device_id_type=MESH
        )

    f32 = jnp.float32
    bf16 = jnp.bfloat16
    chunks = -(-points // LANES)
    slabs = waves.shape[1] // WIDE
    face_chunks = face_send.shape[3] // LANES
    part_rows = left.shape[0] // 2
    cols = elems // n_event
    tile = (8, LANES)

    def lanes_of(k):
        return slice(k * LANES, (k + 1) * LANES)

    rows[...] = jnp.full(rows.shape, -1, jnp.int32)
    waves[...] = jnp.zeros_like(waves)
    before[...] = jnp.zeros_like(before)
    scale_all[...] = jnp.zeros_like(scale_all)
    kappa_buf[...] = jnp.zeros_like(kappa_buf)
    mu_buf[...] = jnp.zeros_like(mu_buf)
    force_buf[...] = jnp.zeros_like(force_buf)
    for i in (4, 5, 6, 10):
        loads[i].wait()
    rows[0:elems, 0:125] = conn[...]
    rows[elems : elems + 1, :] = receivers[...]
    for which, ref in enumerate((lower, upper)):
        for k in range(face_chunks):
            size = min(LANES, face - k * LANES)
            at = elems + 1 + which * face_chunks + k
            rows[at : at + 1, 0:size] = ref[:, k * LANES : k * LANES + size]
    columns = (rows[...].astype(f32).T.astype(jnp.int32) & (WIDE - 1)).astype(f32).astype(bf16)

    lane = lax.broadcasted_iota(jnp.int32, (LANES, WIDE), 1).astype(f32).astype(bf16)
    one = jnp.ones((LANES, WIDE), bf16)
    none = jnp.zeros((LANES, WIDE), bf16)
    half = lax.broadcasted_iota(jnp.int32, (16, LANES), 0) >> 3
    empty = jnp.zeros((16, LANES), bf16)

    def spread(at):
        low = jnp.broadcast_to(columns[:, at : at + 1], (LANES, WIDE))
        onehot[at * LANES : (at + 1) * LANES, :] = jnp.where(lane == low, one, none)

    def take(table, low):
        return jnp.take_along_axis(table, low, axis=1, mode="promise_in_bounds")

    def lookup(tables, index, count):
        low = index & (LANES - 1)
        high = index >> 7
        outs = [jnp.zeros(index.shape, f32) for _ in tables]
        for k in range(count):
            here = high == k
            for t, table in enumerate(tables):
                outs[t] = jnp.where(here, take(table(k), low), outs[t])
        return outs

    def row_of(ref, c):
        return lambda k: jnp.broadcast_to(ref[c : c + 1, lanes_of(k)], tile)

    def place(at, value):
        high = jnp.broadcast_to(rows[at : at + 1, :] >> 8, (16, LANES)) - half
        high = high.astype(f32).astype(bf16)
        parts = two_parts(jnp.concatenate([value, value], 0))
        for k in range(part_rows // 16):
            here = high == jnp.full((16, LANES), 2 * k, bf16)
            for s, part in enumerate(parts):
                row = s * part_rows + 16 * k
                left[row : row + 16, lanes_of(at)] = jnp.where(here, part, empty)

    def deposit(start, stop, out):
        span = slice(start * LANES, stop * LANES)
        total = jnp.dot(left[:, span], onehot[span, :], preferred_element_type=f32)
        total = total[0:part_rows] + total[part_rows:]
        for k in range(slabs):
            out[:, k * WIDE : (k + 1) * WIDE] = total[8 * k : 8 * k + 8]

    def finish(copies):
        @pl.when(has_previous)
        def _():
            copies[0].wait_send()
            copies[1].wait_recv()

        @pl.when(has_following)
        def _():
            copies[1].wait_send()
            copies[0].wait_recv()

    def element_index(group):
        return rows[group * 8 : group * 8 + 8, :]

    def at_elements(ref):
        parts = [[] for _ in range(6)]
        for group in range(elems // 8):
            got = lookup([row_of(ref, c) for c in range(6)], element_index(group), chunks)
            for c in range(6):
                parts[c].append(got[c])
        return parts

    for i in (0, 2):
        loads[i].wait()
    for c in range(3):
        waves[c : c + 1, 0:points] = fwd_now[c]
        waves[3 + c : 4 + c, 0:points] = adj_now[c]
    parts = at_elements(waves)
    for e in range(elems + 1):
        spread(e)
    for i in (12, 7, 8):
        loads[i].wait()
    kappa_buf[:, 0:125] = bulk_mod[...]
    mu_buf[:, 0:125] = shear_mod[...]
    kappa = kappa_buf[...]
    mu = mu_buf[...]

    span = ahead.shape[0] // 3
    forward_table = jnp.concatenate([ahead[i * span : (i + 1) * span, :] for i in range(3)], 1)
    bulk = jnp.zeros((elems, LANES), f32)
    shear = jnp.zeros((elems, LANES), f32)
    pending = []
    for step in range(STEPS):
        values = jnp.concatenate([piece for part in parts for piece in part], 0)
        grads = product(values, forward_table)

        def grad(i, c):
            return grads[c * elems : (c + 1) * elems, i * LANES : (i + 1) * LANES]

        divs, devs = [], []
        for f in range(2):
            g = [[grad(i, f * 3 + j) for j in range(3)] for i in range(3)]
            div = g[0][0] + g[1][1] + g[2][2]
            third = div * (1.0 / 3.0)
            dev = {(i, i): g[i][i] - third for i in range(3)}
            for i, j in ((0, 1), (0, 2), (1, 2)):
                dev[i, j] = 0.5 * (g[i][j] + g[j][i])
            divs.append(div)
            devs.append(dev)
            pressure = kappa * div
            for (i, j), term in dev.items():
                tension = 2.0 * mu * term
                if i == j:
                    tension = tension + pressure
                for first, second in ((i, j), (j, i))[: 1 + (i != j)]:
                    c = f * 3 + second
                    stress_buf[c * elems : (c + 1) * elems, lanes_of(first)] = tension

        bulk = bulk - KERNEL_WEIGHT * kappa * divs[0] * divs[1]
        both = {key: devs[0][key] * devs[1][key] for key in devs[0]}
        paired = both[0, 0] + both[1, 1] + both[2, 2]
        paired = paired + 2.0 * (both[0, 1] + both[0, 2] + both[1, 2])
        shear = shear - 2.0 * KERNEL_WEIGHT * mu * paired

        if step == STEPS - 1:
            for owner in range(n_event):
                kern_send[owner, 0] = bulk[owner * cols : (owner + 1) * cols]
                kern_send[owner, 1] = shear[owner * cols : (owner + 1) * cols]
            for hop in range(1, n_event):
                peer = lax.rem(my_event + hop, n_event)
                copy = pltpu.make_async_remote_copy(
                    src_ref=kern_send.at[peer],
                    dst_ref=kern_recv.at[hop - 1],
                    send_sem=kern_ssem.at[hop - 1],
                    recv_sem=kern_rsem.at[hop - 1],
                    device_id={"mesh": me, "event": peer},
                    device_id_type=MESH,
                )
                copy.start()
                pending.append(copy)

        if step == 0:
            loads[13].wait()
        force_buf[0 : 6 * elems, :] = product(stress_buf[...], back[...])
        for e in range(elems):
            place(e, force_buf[pl.ds(e, 8, stride=elems), :])
        if step == 0:
            loads[11].wait()
        injected = jnp.concatenate(
            [jnp.zeros((3, LANES), f32), source[0, :, step, :], jnp.zeros((2, LANES), f32)], 0
        )
        place(elems, injected)
        deposit(0, elems + 1, forces)

        copies = []
        if step == 0:
            pl.semaphore_wait(barrier, 2 + n_event - 1)
        for which, other in ((0, previous), (1, following)):
            for k in range(face_chunks):
                at = elems + 1 + which * face_chunks + k
                index = jnp.broadcast_to(rows[at : at + 1, :], tile)
                face_send[step, which, :, lanes_of(k)] = lookup(
                    [lambda q: forces[:, lanes_of(q)]], index, chunks
                )[0]
            copy = pltpu.make_async_remote_copy(
                src_ref=face_send.at[step, which],
                dst_ref=face_recv.at[step, 1 - which],
                send_sem=face_ssem.at[step, which],
                recv_sem=face_rsem.at[step, 1 - which],
                device_id={"mesh": other, "event": my_event},
                device_id_type=MESH,
            )
            copies.append(copy)
        pl.when(has_previous)(copies[0].start)
        pl.when(has_following)(copies[1].start)

        if step == 0:
            for i in (1, 3, 9):
                loads[i].wait()
            for c in range(3):
                before[c : c + 1, 0:points] = fwd_prev[c]
                before[3 + c : 4 + c, 0:points] = adj_prev[c]
            scale_all[:, 0:points] = jnp.broadcast_to(scale[...].reshape(1, points), (8, points))
            later[...] = 2.0 * waves[...] - before[...] + scale_all[...] * forces[...]
            parts = at_elements(later)
            number = lax.broadcasted_iota(jnp.int32, tile, 1)
            for which, inside in ((0, has_previous), (1, has_following)):
                for k in range(face_chunks):
                    at = elems + 1 + which * face_chunks + k
                    spread(at)
                    slot = number + ((which * face_chunks + k) * LANES + 1)
                    place(at, jnp.where(inside, slot.astype(f32), 0.0))
            deposit(elems + 1, elems + 1 + 2 * face_chunks, slots)
            found = [
                lookup([row_of(slots, 0)], element_index(group), chunks)[0]
                for group in range(elems // 8)
            ]
            factors = lookup([row_of(scale_all, 0)], rows[elems : elems + 8, :], chunks)[0]
            finish(copies)
            for which in range(2):
                for k in range(face_chunks):
                    at = 1 + which * face_chunks + k
                    span = lanes_of(k)
                    face_scaled[which, :, span] = (
                        face_recv[step, which, :, span] * factors[at : at + 1, :]
                    )
            for group in range(elems // 8):
                which = 0 if group < elems // 16 else 1
                index = found[group].astype(jnp.int32) - (1 + which * face_chunks * LANES)
                got = lookup(
                    [row_of(face_scaled.at[which], c) for c in range(6)], index, face_chunks
                )
                for c in range(6):
                    parts[c][group] = parts[c][group] + got[c]
        else:

            def arrived(at, q):
                index = slots[:, lanes_of(q)].astype(jnp.int32) - 1
                return lookup(
                    [
                        lambda k: face_recv[
                            at, k // face_chunks, :, lanes_of(k % face_chunks)
                        ]
                    ],
                    index,
                    2 * face_chunks,
                )[0]

            for q in range(chunks):
                span = lanes_of(q)
                now = later[:, span] + scale_all[:, span] * arrived(0, q)
                before[:, span] = (
                    2.0 * now - waves[:, span] + scale_all[:, span] * forces[:, span]
                )
            finish(copies)
            for q in range(chunks):
                span = lanes_of(q)
                later[:, span] = before[:, span] + scale_all[:, span] * arrived(1, q)

    for c in range(3):
        fwd_out[c] = later[c : c + 1, 0:points]
        adj_out[c] = later[3 + c : 4 + c, 0:points]
    owned = kern_send[my_event]
    for copy in pending:
        copy.wait()
    for hop in range(1, n_event):
        owned = owned + kern_recv[hop - 1]
    kern_out[...] = owned[:, :, 0:125]


def copy_out(*refs):
    count = len(refs) // 2
    sem = refs[-1]
    copies = [pltpu.make_async_copy(refs[i], refs[count + i], sem.at[i]) for i in range(count)]
    for copy in copies:
        copy.start()
    for copy in copies:
        copy.wait()


def hand_out(results):
    count = len(results)
    return pl.pallas_call(
        copy_out,
        out_shape=tuple(jax.ShapeDtypeStruct(v.shape, v.dtype) for v in results),
        in_specs=[pl.BlockSpec(memory_space=pltpu.VMEM)] * count,
        out_specs=[pl.BlockSpec(memory_space=pltpu.HBM)] * count,
        scratch_shapes=[pltpu.SemaphoreType.DMA((count,))],
        compiler_params=pltpu.CompilerParams(vmem_limit_bytes=1024 * 1024),
    )(*results)


def shards(
    n_mesh,
    n_event,
    forward_now,
    forward_prev,
    adjoint_now,
    adjoint_prev,
    connectivity,
    lower_face,
    upper_face,
    bulk_modulus,
    shear_modulus,
    step_scale,
    receiver_points,
    adjoint_source,
):
    points = forward_now.shape[2]
    face = lower_face.shape[1]
    elems = connectivity.shape[1]
    cols = elems // n_event
    slabs = -(-points // WIDE)
    slabs += slabs % 2
    width = slabs * WIDE
    face_chunks = -(-face // LANES)
    blocks = elems + 1 + 2 * face_chunks
    f32 = jnp.float32
    ahead, back = cube_tables()
    fields = [v.transpose(1, 0, 2) for v in (forward_now, forward_prev, adjoint_now, adjoint_prev)]
    operands = (
        *fields,
        connectivity.T,
        lower_face,
        upper_face,
        bulk_modulus.T,
        shear_modulus.T,
        step_scale,
        receiver_points.reshape(1, -1),
        adjoint_source.transpose(0, 2, 1, 3),
        jnp.asarray(np.concatenate(np.split(ahead, 3, 1), 0)),
        jnp.asarray(back),
    )
    state = pltpu.VMEM((8, width), f32)
    moduli = pltpu.VMEM((elems, LANES), f32)
    peers = max(n_event - 1, 1)
    call = pl.pallas_call(
        functools.partial(body, n_mesh, n_event, points, face, elems),
        out_shape=(
            pltpu.VMEM(fields[0].shape, f32),
            pltpu.VMEM(fields[2].shape, f32),
            pltpu.VMEM((2, cols, 125), f32),
        ),
        in_specs=[pl.BlockSpec(memory_space=pltpu.HBM)] * 14,
        out_specs=[pl.BlockSpec(memory_space=pltpu.VMEM)] * 3,
        scratch_shapes=[
            *[pltpu.VMEM(v.shape, v.dtype) for v in operands],
            pltpu.SemaphoreType.DMA((14,)),
            state,
            state,
            state,
            state,
            state,
            state,
            moduli,
            moduli,
            pltpu.VMEM((LANES, LANES), jnp.int32),
            pltpu.VMEM((blocks * LANES, WIDE), jnp.bfloat16),
            pltpu.VMEM((2 * slabs * 8, blocks * LANES), jnp.bfloat16),
            pltpu.VMEM((6 * elems, 3 * LANES), f32),
            pltpu.VMEM((8 * elems, LANES), f32),
            pltpu.VMEM((STEPS, 2, 8, face_chunks * LANES), f32),
            pltpu.VMEM((STEPS, 2, 8, face_chunks * LANES), f32),
            pltpu.VMEM((2, 8, face_chunks * LANES), f32),
            pltpu.VMEM((n_event, 2, cols, LANES), f32),
            pltpu.VMEM((peers, 2, cols, LANES), f32),
            pltpu.SemaphoreType.DMA((STEPS, 2)),
            pltpu.SemaphoreType.DMA((STEPS, 2)),
            pltpu.SemaphoreType.DMA((peers,)),
            pltpu.SemaphoreType.DMA((peers,)),
        ],
        compiler_params=pltpu.CompilerParams(
            collective_id=0, has_side_effects=True, vmem_limit_bytes=60 * 1024 * 1024
        ),
    )
    forward, adjoint, kernels = hand_out(call(*operands))
    return (forward.transpose(1, 0, 2), adjoint.transpose(1, 0, 2), kernels.transpose(0, 2, 1))


def solution(mesh):
    placed = (
        P("event", None, "mesh"),
        P("event", None, "mesh"),
        P("event", None, "mesh"),
        P("event", None, "mesh"),
        P(None, "mesh"),
        P("mesh", None),
        P("mesh", None),
        P(None, "mesh"),
        P(None, "mesh"),
        P("mesh"),
        P("mesh"),
        P("event", None, None, "mesh"),
    )
    return jax.shard_map(
        functools.partial(shards, mesh.shape["mesh"], mesh.shape["event"]),
        mesh=mesh,
        in_specs=placed,
        out_specs=(
            P("event", None, "mesh"),
            P("event", None, "mesh"),
            P(None, None, ("mesh", "event")),
        ),
        check_vma=False,
    )
```
